256 devices in a mesh: space: 16 (over z, y_hi), band: 16 (over x, y_lo, core).
Axes of the slice: x: 4, y: 4 (y_hi: 2, y_lo: 2; y = y_hi * 2 + y_lo), z: 8, core: 2. Of those that a mesh axis runs over, the one named last changes fastest.
Arguments:
- columns: float32 [64, 96, 32, 128], P('band', 'space'), may hold values from -6 to 6
- potential: float32 [96, 32, 128], P('space'), may hold values from -1 to 3
- orbitals: float32 [512, 96, 32, 128], P('band', 'space'), may hold values from -0.0390625 to 0.0390625
Outputs:
- projected: float32 [64, 96, 32, 128], P('band', 'space')
- correlation: float32 [512, 64], P('band')
The draws below stay inside these ranges and needn't reach their ends.
All inputs are finite; a program needn't handle non-finite values.
Results may differ from the reference program's by a relative error of at most 0.00011.
Values sent between devices are 32-bit elements; how exact they have to be, the bound alone decides.
A program may use at most 64 MiB of HBM per device.

```python
import jax
import jax.numpy as jnp
from jax import lax

NY = 32
NX = 128
ORBS = 512
NZ = 96
COLS = 64


def steps_of(key, dims, cuts, low, high):
    factor_of = 1.0
    for axis_at, blocks in cuts:
        heights = jax.random.uniform(jax.random.fold_in(jax.random.fold_in(key, 6), axis_at), (blocks,), jnp.float32, low / len(cuts), high / len(cuts))
        factor_of = factor_of * jnp.repeat(jnp.exp(heights), dims[axis_at] // blocks).reshape((-1,) + (1,) * (len(dims) - 1 - axis_at))
    return factor_of


def centred(own_key, shape, deviation, limit, split=(), kind=jnp.bfloat16):
    level = steps_of(own_key, shape, split, -0.22, 0.18) if split else 1.0
    values = jax.random.normal(own_key, shape, jnp.float32) * deviation * level
    return jnp.minimum(jnp.maximum(values, -limit), limit).astype(kind)


def setup_inputs(seed: int = 0) -> dict:
    keys = jax.random.split(jax.random.key(seed), 4)
    return {
        "columns": centred(keys[0], (COLS, NZ, NY, NX), 1.0, 6.0, ((0, 16), (1, 16)), jnp.float32),
        "potential": jnp.clip(-1.0 + 4.0 * jax.random.uniform(keys[1], (NZ, NY, NX), jnp.float32) ** steps_of(keys[1], (NZ, NY, NX), ((0, 16),), -0.2, 0.2), -1.0, 3.0),
        "orbitals": centred(keys[2], (ORBS, NZ, NY, NX), (NZ * NY * NX // 16) ** -0.5, 0.0390625, ((0, 16), (1, 16)), jnp.float32),
    }


COEFFS = (-5369.0 / 1800.0, 12.0 / 7.0, -15.0 / 56.0, 10.0 / 189.0, -1.0 / 112.0, 2.0 / 1925.0, -1.0 / 16632.0)


def hamiltonian(values, potential):
    laplace = 3.0 * COEFFS[0] * values
    for offset in range(1, 7):
        along = jnp.roll(values, offset, 1) + jnp.roll(values, -offset, 1)
        along = along + jnp.roll(values, offset, 2) + jnp.roll(values, -offset, 2)
        along = along + jnp.roll(values, offset, 3) + jnp.roll(values, -offset, 3)
        laplace = laplace + COEFFS[offset] * along
    return -0.5 * laplace + potential[None] * values


def reference(columns, potential, orbitals):
    applied = hamiltonian(columns, potential)
    psi_flat = orbitals.reshape(orbitals.shape[0], -1)
    applied_flat = applied.reshape(applied.shape[0], -1)
    correlation = jnp.einsum("oc,kc->ok", psi_flat, applied_flat, precision=lax.Precision.HIGHEST)
    removed = jnp.einsum("ok,oc->kc", correlation, psi_flat, precision=lax.Precision.HIGHEST)
    projected = (applied_flat - removed).reshape(applied.shape)
    return projected, correlation
```

```python
import jax
import jax.numpy as jnp
from jax import lax
from jax.experimental import pallas as pl
from jax.experimental.pallas import tpu as pltpu
from jax.sharding import PartitionSpec as P

COEFFS = (
    -5369.0 / 1800.0,
    12.0 / 7.0,
    -15.0 / 56.0,
    10.0 / 189.0,
    -1.0 / 112.0,
    2.0 / 1925.0,
    -1.0 / 16632.0,
)

MESH = pl.DeviceIdType.MESH
NZ_RING, NX_RING = 8, 4
COLS, ORBS = 4, 32
PLANES, NY, NX = 6, 32, 128
ROWS = PLANES * NY
PART = ROWS // 8

STEPS = ((0, 0), (0, 1), (1, 0), (1, 1), (3, 0), (3, 1), (2, 0), (2, 1))


def kernel(
    col_hbm, pot_ref, orb_hbm, proj_ref, corr_ref,
    colv, halo, app, phibuf, phi, acol, ahl, cpart, cin, zin, ctot, cts,
    rsend, rrecv, rown, fin, rem,
    loc_sem, orb_s, orb_r, halo_s, halo_r, col_s, col_r, fwd_s, fwd_r,
    s1_s, s1_r, s2_s, s2_r, s3_s, s3_r, ry_s, ry_r, fin_s, fin_r,
):
    s, b = lax.axis_index("space"), lax.axis_index("band")
    z, h = s // 2, s % 2
    x, yl, c = b // 4, (b // 2) % 2, b % 2
    me = x * 2 + c

    def dev(dz=0, dh=0, dx=0, dy=0, dc=0):
        return (
            ((z + dz) % NZ_RING) * 2 + (h + dh) % 2,
            ((x + dx) % NX_RING) * 4 + ((yl + dy) % 2) * 2 + (c + dc) % 2,
        )

    def part_of(dx, dc):
        return ((x + dx) % NX_RING) * 2 + (c + dc) % 2

    def rows_of(g):
        return pl.ds(pl.multiple_of(g * PART, PART), PART)

    def slot_of(side, g):
        return pl.ds((side * 8 + g) * COLS, COLS)

    after, before = ((s + 1) % 16, b), ((s + 15) % 16, b)
    partner = dev(dy=1)

    barrier = pltpu.get_barrier_semaphore()
    peers = [dev(dx=dx, dc=dc, dh=dh) for dh in (0, 1) for dx, dc in STEPS if (dx, dc, dh) != (0, 0, 0)]
    peers += [dev(dz=dz) for dz in range(1, NZ_RING)]
    far_slab = (((s + 15) % 16) * (1 - h) + ((s + 1) % 16) * h, b)
    peers += [partner, far_slab]
    for peer in peers:
        pl.semaphore_signal(barrier, inc=1, device_id=peer, device_id_type=MESH)

    load_col = pltpu.make_async_copy(col_hbm, colv, loc_sem.at[0])
    load_col.start()
    load_orb = pltpu.make_async_copy(orb_hbm.at[:, rows_of(me), :], phibuf.at[pl.ds(0, ORBS)], loc_sem.at[1])
    load_orb.start()

    pl.semaphore_wait(barrier, len(peers))

    halos = [
        pltpu.make_async_remote_copy(
            col_hbm, halo.at[i], halo_s.at[i], halo_r.at[i], device_id=to, device_id_type=MESH
        )
        for i, to in ((0, after), (1, before))
    ]
    for copy in halos:
        copy.start()
    orbs = {}
    for i, (dx, dc) in enumerate(STEPS):
        if i > 0:
            orbs[i] = pltpu.make_async_remote_copy(
                orb_hbm.at[:, rows_of(part_of(dx, dc)), :],
                phibuf.at[pl.ds(i * ORBS, ORBS)],
                orb_s.at[i],
                orb_r.at[i],
                device_id=dev(dx=dx, dc=dc),
                device_id_type=MESH,
            )
    for i in (1, 2, 4, 3, 5, 6):
        orbs[i].start()

    load_col.wait()

    def local_terms(j, carry):
        planes = [colv[j, pl.ds(p * NY, NY), :] for p in range(PLANES)]
        for p in range(PLANES):
            v = planes[p]
            total = (pot_ref[pl.ds(p * NY, NY), :] - 1.5 * COEFFS[0]) * v
            for k in range(1, 7):
                along = pltpu.roll(v, k, 0) + pltpu.roll(v, NY - k, 0)
                along = along + (pltpu.roll(v, k, 1) + pltpu.roll(v, NX - k, 1))
                if p - k >= 0:
                    along = along + planes[p - k]
                if p + k < PLANES:
                    along = along + planes[p + k]
                total = total + (-0.5 * COEFFS[k]) * along
            app[j, pl.ds(p * NY, NY), :] = total
        return carry

    lax.fori_loop(0, COLS, local_terms, 0)

    def lay_out(i0, n):
        def one(q, carry):
            value = phibuf[pl.ds(i0 * ORBS, n * ORBS), q, :]
            high = value.astype(jnp.bfloat16)
            low = (value - high.astype(jnp.float32)).astype(jnp.bfloat16)
            at = pl.ds(pl.multiple_of(q * NX, NX), NX)
            phi[0, pl.ds(i0 * ORBS, n * ORBS), at] = high
            phi[1, pl.ds(i0 * ORBS, n * ORBS), at] = low
            return carry

        lax.fori_loop(0, PART, one, 0)

    load_orb.wait()
    orbs[1].wait_recv()
    lay_out(0, 2)

    for copy in halos:
        copy.wait_recv()

    def halo_terms(j, carry):
        for p in range(PLANES):
            total = app[j, pl.ds(p * NY, NY), :]
            for k in range(1, 7):
                if p - k < 0:
                    total = total + (-0.5 * COEFFS[k]) * halo[0, j, pl.ds((p - k + PLANES) * NY, NY), :]
                if p + k >= PLANES:
                    total = total + (-0.5 * COEFFS[k]) * halo[1, j, pl.ds((p + k - PLANES) * NY, NY), :]
            app[j, pl.ds(p * NY, NY), :] = total
        return carry

    lax.fori_loop(0, COLS, halo_terms, 0)

    own_col = pltpu.make_async_copy(app.at[:, rows_of(me), :], acol.at[slot_of(yl, me)], loc_sem.at[2])
    own_col.start()
    cols, fwds = {}, {}
    for i, (dx, dc) in enumerate(STEPS):
        if i > 0:
            cols[i] = pltpu.make_async_remote_copy(
                app.at[:, rows_of(part_of(dx, dc)), :],
                acol.at[slot_of(yl, me)],
                col_s.at[i],
                col_r.at[i],
                device_id=dev(dx=dx, dc=dc),
                device_id_type=MESH,
            )
        came = slot_of(yl, part_of(-dx, -dc))
        fwds[i] = pltpu.make_async_remote_copy(
            app.at[:, rows_of(me), :] if i == 0 else acol.at[came],
            acol.at[came],
            fwd_s.at[i],
            fwd_r.at[i],
            device_id=partner,
            device_id_type=MESH,
        )
    for i in (6, 7, 2, 4, 3, 5, 1):
        cols[i].start()
    fwds[0].start()
    orbs[7].start()
    for i in (1, 2, 4, 3, 5, 6, 7):
        cols[i].wait_recv()
        fwds[i].start()

    for i in (2, 3, 4, 5):
        orbs[i].wait_recv()
    lay_out(2, 4)

    own_col.wait()
    for i in range(8):
        fwds[i].wait_recv()

    def lay_out_columns(q, carry):
        value = acol[:, q, :]
        high = value.astype(jnp.bfloat16)
        low = (value - high.astype(jnp.float32)).astype(jnp.bfloat16)
        at = pl.ds(pl.multiple_of(q * NX, NX), NX)
        ahl[pl.ds(0, 64), at] = high
        ahl[pl.ds(64, 64), at] = low
        return carry

    lax.fori_loop(0, PART, lay_out_columns, 0)

    half_lanes = lax.broadcasted_iota(jnp.int32, (16, 128), 1) < 64
    dims = (((1,), (1,)), ((), ()))

    def correlate(i0, n):
        rows = pl.ds(i0 * ORBS, n * ORBS)
        high = lax.dot_general(phi[0, rows, :], ahl[...], dims, preferred_element_type=jnp.float32)
        low = lax.dot_general(phi[1, rows, :], ahl[...], dims, preferred_element_type=jnp.float32)
        value = high + pltpu.roll(high, 64, 1) + low
        for i in range(n):
            first = value[i * ORBS : i * ORBS + 16]
            second = value[i * ORBS + 16 : i * ORBS + 32]
            packed = jnp.where(half_lanes, first, pltpu.roll(second, 64, 1))
            cpart[i0 + i, 0] = packed[:8]
            cpart[i0 + i, 1] = packed[8:]

    sums = {}

    def send_parts(i):
        dx, dc = STEPS[i]
        for dh in (0, 1):
            if (i, dh) != (0, 0):
                n = i * 2 + dh
                sums[n] = pltpu.make_async_remote_copy(
                    cpart.at[i, (h + dh) % 2],
                    cin.at[n],
                    s1_s.at[n],
                    s1_r.at[n],
                    device_id=dev(dx=-dx, dc=-dc, dh=dh),
                    device_id_type=MESH,
                )
                sums[n].start()

    correlate(0, 6)
    for i in (2, 4, 3, 5, 1, 0):
        send_parts(i)
    for i in (6, 7):
        orbs[i].wait_recv()
    lay_out(6, 2)
    correlate(6, 2)
    send_parts(6)
    send_parts(7)

    total = cpart[0, h]
    for n in range(1, 16):
        sums[n].wait_recv()
        total = total + cin[n]

    zin[z] = total
    zs = []
    for dz in (4, 3, 5, 2, 6, 1, 7):
        copy = pltpu.make_async_remote_copy(
            zin.at[z], zin.at[z], s2_s.at[dz], s2_r.at[dz], device_id=dev(dz=dz), device_id_type=MESH
        )
        copy.start()
        zs.append(copy)
    for copy in zs:
        copy.wait_recv()
    total = zin[0]
    for n in range(1, NZ_RING):
        total = total + zin[n]

    ctot[0, h] = total
    backs = []
    for i in (6, 7, 2, 4, 3, 5, 1, 0):
        dx, dc = STEPS[i]
        for dh in (1, 0):
            if (i, dh) != (0, 0):
                n = i * 2 + dh
                copy = pltpu.make_async_remote_copy(
                    ctot.at[0, h],
                    ctot.at[i, h],
                    s3_s.at[n],
                    s3_r.at[n],
                    device_id=dev(dx=dx, dc=dc, dh=dh),
                    device_id_type=MESH,
                )
                copy.start()
                backs.append(copy)
    for copy in backs:
        copy.wait_recv()

    packed = ctot[...].reshape(8, 16, 128)
    swapped = pltpu.roll(packed.reshape(128, 128), 64, 1).reshape(8, 16, 128)
    corr = jnp.concatenate([packed, swapped], axis=1).reshape(256, 128)
    flat = jnp.transpose(corr)[:64]
    high = flat.astype(jnp.bfloat16)
    low = (flat - high.astype(jnp.float32)).astype(jnp.bfloat16)
    for side in (0, 1):
        cts[side, pl.ds(0, 32), :] = high[side * 32 : side * 32 + 32]
        cts[side, pl.ds(32, 32), :] = low[side * 32 : side * 32 + 32]

    def removed(side, out):
        for q0 in range(0, PART, 4):
            at = pl.ds(q0 * NX, 4 * NX)
            both = jnp.dot(cts[side], phi[0, :, at], preferred_element_type=jnp.float32)
            rest = jnp.dot(cts[side, pl.ds(0, 32), :], phi[1, :, at], preferred_element_type=jnp.float32)
            value = both[:32] + both[32:] + rest
            for q in range(4):
                for k in range(NX_RING):
                    out[k, q0 + q] = value[k * 8 : k * 8 + 8, q * NX : (q + 1) * NX]

    removed(1 - yl, rsend)
    order = (2, 1, 3, 0)
    ys = {}
    for dx in order:
        k = (x + dx) % NX_RING
        ys[dx] = pltpu.make_async_remote_copy(
            rsend.at[k], rrecv.at[k], ry_s.at[dx], ry_r.at[dx], device_id=partner, device_id_type=MESH
        )
        ys[dx].start()
    removed(yl, rown)

    own = corr[:32]
    lane = lax.broadcasted_iota(jnp.int32, (ORBS, 128), 1)
    value = own
    for side in (0, 1):
        for k in range(NX_RING):
            source, target = side * 32 + k * 8, k * 16 + side * 8
            if source != target:
                moved = pltpu.roll(own, (target - source) % 128, 1)
                value = jnp.where((lane >= target) & (lane < target + 8), moved, value)
    corr_ref[...] = value[:, :64]

    fins = {}
    for dx in order:
        k = (x + dx) % NX_RING
        ys[dx].wait_recv()
        for j in range(8):
            fin[k, j] = rown[k, :, j, :] + rrecv[k, :, j, :]
        for dc in (1, 0):
            source = fin.at[k, pl.ds(((c + dc) % 2) * COLS, COLS)]
            target = rem.at[:, rows_of(me), :]
            n = STEPS.index((dx, dc))
            if n == 0:
                local = pltpu.make_async_copy(source, target, loc_sem.at[3])
                local.start()
            else:
                fins[n] = pltpu.make_async_remote_copy(
                    source, target, fin_s.at[n], fin_r.at[n], device_id=dev(dx=dx, dc=dc), device_id_type=MESH
                )
                fins[n].start()
    local.wait()
    for copy in fins.values():
        copy.wait_recv()
    proj_ref[...] = app[...] - rem[...]

    for group in (halos, orbs.values(), cols.values(), fwds.values(), sums.values(), zs, backs, ys.values(), fins.values()):
        for copy in group:
            copy.wait_send()


def shards(columns, potential, orbitals):
    f32, bf16 = jnp.float32, jnp.bfloat16
    dma = pltpu.SemaphoreType.DMA
    scratch = [
        pltpu.VMEM((COLS, ROWS, NX), f32),
        pltpu.VMEM((2, COLS, ROWS, NX), f32),
        pltpu.VMEM((COLS, ROWS, NX), f32),
        pltpu.VMEM((8 * ORBS, PART, NX), f32),
        pltpu.VMEM((2, 8 * ORBS, PART * NX), bf16),
        pltpu.VMEM((64, PART, NX), f32),
        pltpu.VMEM((128, PART * NX), bf16),
        pltpu.VMEM((8, 2, 8, 128), f32),
        pltpu.VMEM((16, 8, 128), f32),
        pltpu.VMEM((NZ_RING, 8, 128), f32),
        pltpu.VMEM((8, 2, 8, 128), f32),
        pltpu.VMEM((2, 64, 256), bf16),
        pltpu.VMEM((NX_RING, PART, 8, NX), f32),
        pltpu.VMEM((NX_RING, PART, 8, NX), f32),
        pltpu.VMEM((NX_RING, PART, 8, NX), f32),
        pltpu.VMEM((NX_RING, 8, PART, NX), f32),
        pltpu.VMEM((COLS, ROWS, NX), f32),
        dma((4,)),
        dma((8,)), dma((8,)),
        dma((2,)), dma((2,)),
        dma((8,)), dma((8,)),
        dma((8,)), dma((8,)),
        dma((16,)), dma((16,)),
        dma((8,)), dma((8,)),
        dma((16,)), dma((16,)),
        dma((4,)), dma((4,)),
        dma((8,)), dma((8,)),
    ]
    vmem, anywhere = pl.BlockSpec(memory_space=pltpu.VMEM), pl.BlockSpec(memory_space=pl.ANY)
    projected, correlation = pl.pallas_call(
        kernel,
        out_shape=(
            jax.ShapeDtypeStruct((COLS, ROWS, NX), f32),
            jax.ShapeDtypeStruct((ORBS, 64), f32),
        ),
        in_specs=[anywhere, vmem, anywhere],
        out_specs=(vmem, vmem),
        scratch_shapes=scratch,
        compiler_params=pltpu.CompilerParams(
            collective_id=0, has_side_effects=True, vmem_limit_bytes=40 * 2**20
        ),
        name="sternheimer",
    )(
        columns.reshape(COLS, ROWS, NX),
        potential.reshape(ROWS, NX),
        orbitals.reshape(ORBS, ROWS, NX),
    )
    return projected.reshape(columns.shape), correlation


def solution(mesh):
    placed = (
        P("band", "space", None, None),
        P("space", None, None),
        P("band", "space", None, None),
    )
    return jax.shard_map(
        shards,
        mesh=mesh,
        in_specs=placed,
        out_specs=(P("band", "space", None, None), P("band", None)),
        check_vma=False,
    )
```

```python
import jax
import jax.numpy as jnp
from jax import lax
from jax.experimental import pallas as pl
from jax.experimental.pallas import tpu as pltpu
from jax.sharding import PartitionSpec as P

COEFFS = (
    -5369.0 / 1800.0,
    12.0 / 7.0,
    -15.0 / 56.0,
    10.0 / 189.0,
    -1.0 / 112.0,
    2.0 / 1925.0,
    -1.0 / 16632.0,
)

MESH = pl.DeviceIdType.MESH
NZ_RING, NX_RING = 8, 4
COLS, ORBS = 4, 32
PLANES, NY, NX = 6, 32, 128
ROWS = PLANES * NY
PART = ROWS // 8

STEPS = ((0, 0), (0, 1), (1, 0), (1, 1), (3, 0), (3, 1), (2, 0), (2, 1))


def kernel(
    col_hbm, pot_hbm, orb_hbm, proj_ref, corr_ref,
    colv, potv, relay, halo, app, phibuf, phi, acol, ahl, cpart, cin, zin, ctot, cts,
    rsend, rrecv, rown, fin, rem,
    loc_sem, near_sem, orb_s, orb_r, h1_s, h1_r, h2_s, h2_r, h3_s, h3_r, col_s, col_r, fwd_s, fwd_r,
    s1_s, s1_r, s2_s, s2_r, s3_s, s3_r, ry_s, ry_r, fin_s, fin_r,
):
    s, b = lax.axis_index("space"), lax.axis_index("band")
    z, h = s // 2, s % 2
    x, yl, c = b // 4, (b // 2) % 2, b % 2
    me = x * 2 + c

    def dev(dz=0, dh=0, dx=0, dy=0, dc=0):
        return (
            ((z + dz) % NZ_RING) * 2 + (h + dh) % 2,
            ((x + dx) % NX_RING) * 4 + ((yl + dy) % 2) * 2 + (c + dc) % 2,
        )

    def part_of(dx, dc):
        return ((x + dx) % NX_RING) * 2 + (c + dc) % 2

    def rows_of(g):
        return pl.ds(pl.multiple_of(g * PART, PART), PART)

    def slot_of(side, g):
        return pl.ds((side * 8 + g) * COLS, COLS)

    def along_y(step):
        y = (h * 2 + yl + step + 4) % 4
        return y // 2, (z * 2 + y // 2, x * 4 + (y % 2) * 2 + c)

    def signal(sem, to):
        pl.semaphore_signal(sem, inc=1, device_id=to, device_id_type=MESH)

    partner = dev(dy=1)

    barrier = pltpu.get_barrier_semaphore()
    peers = [dev(dx=dx, dc=dc) for dx, dc in STEPS[1:]]
    peers += [along_y(1)[1], along_y(-1)[1], dev(dz=1), dev(dz=NZ_RING - 1)]
    for peer in peers:
        signal(barrier, peer)

    load_col = pltpu.make_async_copy(col_hbm, colv, loc_sem.at[0])
    load_col.start()
    load_pot = pltpu.make_async_copy(pot_hbm, potv, loc_sem.at[4])
    load_pot.start()
    load_orb = pltpu.make_async_copy(orb_hbm.at[:, rows_of(me), :], phibuf.at[pl.ds(0, ORBS)], loc_sem.at[1])
    load_orb.start()

    pl.semaphore_wait(barrier, len(peers))

    signal(near_sem.at[0], dev(dz=1))
    signal(near_sem.at[1], dev(dz=NZ_RING - 1))
    hop1, hop2, hop3 = [], [], []
    for j in (0, 2, 1, 3):
        step = 1 if j < 2 else -1
        h_to, to = along_y(step)
        hop1.append(
            pltpu.make_async_remote_copy(
                col_hbm.at[j], relay.at[j], h1_s.at[j], h1_r.at[j], device_id=to, device_id_type=MESH
            )
        )
        hop2.append(
            pltpu.make_async_remote_copy(
                relay.at[j], halo.at[1 - h_to, j], h2_s.at[j], h2_r.at[j], device_id=to, device_id_type=MESH
            )
        )
        hop3.append(
            pltpu.make_async_remote_copy(
                halo.at[1 - h, j],
                halo.at[h, j],
                h3_s.at[j],
                h3_r.at[j],
                device_id=(((z + 1 - 2 * h + NZ_RING) % NZ_RING) * 2 + h, b),
                device_id_type=MESH,
            )
        )
        hop1[-1].start()

    orbs = {}
    for i, (dx, dc) in enumerate(STEPS):
        if i > 0:
            orbs[i] = pltpu.make_async_remote_copy(
                orb_hbm.at[:, rows_of(part_of(dx, dc)), :],
                phibuf.at[pl.ds(i * ORBS, ORBS)],
                orb_s.at[i],
                orb_r.at[i],
                device_id=dev(dx=dx, dc=dc),
                device_id_type=MESH,
            )
    for i in (1, 2, 4, 3, 5):
        orbs[i].start()

    load_col.wait()
    load_pot.wait()

    def local_terms(j, carry):
        planes = [colv[j, pl.ds(p * NY, NY), :] for p in range(PLANES)]
        for p in range(PLANES):
            v = planes[p]
            total = (potv[pl.ds(p * NY, NY), :] - 1.5 * COEFFS[0]) * v
            for k in range(1, 7):
                along = pltpu.roll(v, k, 0) + pltpu.roll(v, NY - k, 0)
                along = along + (pltpu.roll(v, k, 1) + pltpu.roll(v, NX - k, 1))
                if p - k >= 0:
                    along = along + planes[p - k]
                if p + k < PLANES:
                    along = along + planes[p + k]
                total = total + (-0.5 * COEFFS[k]) * along
            app[j, pl.ds(p * NY, NY), :] = total
        return carry

    lax.fori_loop(0, COLS, local_terms, 0)

    def split(value):
        high = value.astype(jnp.bfloat16)
        return high, (value - high.astype(jnp.float32)).astype(jnp.bfloat16)

    def lay_out(ref, store, r0, blocks):
        def one(r, carry):
            rows = pl.ds(pl.multiple_of(r0 + r * 16, 16), 16)
            for q0 in range(0, PART, 8):
                high, low = split(jnp.swapaxes(ref[rows, q0 : q0 + 8, :], 0, 1))
                for q in range(8):
                    store(r0 + r * 16, pl.ds((q0 + q) * NX, NX), high[q], low[q])
            return carry

        lax.fori_loop(0, blocks, one, 0)

    def store_orbitals(row, at, high, low):
        rows = pl.ds(pl.multiple_of(row, 16), 16)
        phi[0, rows, at] = high
        phi[1, rows, at] = low

    def store_columns(row, at, high, low):
        ahl[pl.ds(pl.multiple_of(row, 16), 16), at] = high
        ahl[pl.ds(pl.multiple_of(64 + row, 16), 16), at] = low

    for copy, onward in zip(hop1, hop2):
        copy.wait_recv()
        onward.start()
    load_orb.wait()
    orbs[1].wait_recv()
    lay_out(phibuf, store_orbitals, 0, 4)
    for copy, onward in zip(hop2, hop3):
        copy.wait_recv()
        onward.start()
    for i in (0, 1):
        pl.semaphore_wait(near_sem.at[i], 1)
    signal(near_sem.at[2], dev(dz=2))
    signal(near_sem.at[3], dev(dz=NZ_RING - 2))

    for copy in hop3:
        copy.wait_recv()

    def halo_terms(j, carry):
        for p in range(PLANES):
            total = app[j, pl.ds(p * NY, NY), :]
            for k in range(1, 7):
                if p - k < 0:
                    total = total + (-0.5 * COEFFS[k]) * halo[0, j, pl.ds((p - k + PLANES) * NY, NY), :]
                if p + k >= PLANES:
                    total = total + (-0.5 * COEFFS[k]) * halo[1, j, pl.ds((p + k - PLANES) * NY, NY), :]
            app[j, pl.ds(p * NY, NY), :] = total
        return carry

    lax.fori_loop(0, COLS, halo_terms, 0)

    own_col = pltpu.make_async_copy(app.at[:, rows_of(me), :], acol.at[slot_of(yl, me)], loc_sem.at[2])
    own_col.start()
    cols, fwds = {}, {}
    for i, (dx, dc) in enumerate(STEPS):
        if i > 0:
            cols[i] = pltpu.make_async_remote_copy(
                app.at[:, rows_of(part_of(dx, dc)), :],
                acol.at[slot_of(yl, me)],
                col_s.at[i],
                col_r.at[i],
                device_id=dev(dx=dx, dc=dc),
                device_id_type=MESH,
            )
        came = slot_of(yl, part_of(-dx, -dc))
        fwds[i] = pltpu.make_async_remote_copy(
            app.at[:, rows_of(me), :] if i == 0 else acol.at[came],
            acol.at[came],
            fwd_s.at[i],
            fwd_r.at[i],
            device_id=partner,
            device_id_type=MESH,
        )
    for i in (6, 7, 2, 4, 3, 5, 1):
        cols[i].start()
    fwds[0].start()
    orbs[6].start()
    orbs[7].start()
    for i in (1, 2, 4, 3, 5, 6, 7):
        cols[i].wait_recv()
        fwds[i].start()

    for i in (2, 3, 4, 5):
        orbs[i].wait_recv()
    lay_out(phibuf, store_orbitals, 64, 8)

    own_col.wait()
    for i in range(8):
        fwds[i].wait_recv()

    lay_out(acol, store_columns, 0, 4)

    half_lanes = lax.broadcasted_iota(jnp.int32, (16, 128), 1) < 64
    dims = (((1,), (1,)), ((), ()))

    def correlate(i0, n):
        rows = pl.ds(i0 * ORBS, n * ORBS)
        high = lax.dot_general(phi[0, rows, :], ahl[...], dims, preferred_element_type=jnp.float32)
        low = lax.dot_general(phi[1, rows, :], ahl[...], dims, preferred_element_type=jnp.float32)
        value = high + pltpu.roll(high, 64, 1) + low
        for i in range(n):
            first = value[i * ORBS : i * ORBS + 16]
            second = value[i * ORBS + 16 : i * ORBS + 32]
            packed = jnp.where(half_lanes, first, pltpu.roll(second, 64, 1))
            cpart[i0 + i, 0] = packed[:8]
            cpart[i0 + i, 1] = packed[8:]

    sums = {}

    def send_parts(i):
        dx, dc = STEPS[i]
        for dh in (0, 1):
            if (i, dh) != (0, 0):
                n = i * 2 + dh
                sums[n] = pltpu.make_async_remote_copy(
                    cpart.at[i, (h + dh) % 2],
                    cin.at[n],
                    s1_s.at[n],
                    s1_r.at[n],
                    device_id=dev(dx=-dx, dc=-dc, dh=dh),
                    device_id_type=MESH,
                )
                sums[n].start()

    correlate(0, 6)
    for i in (2, 4, 3, 5, 1, 0):
        send_parts(i)
    for i in (6, 7):
        orbs[i].wait_recv()
    lay_out(phibuf, store_orbitals, 192, 4)
    correlate(6, 2)
    send_parts(6)
    send_parts(7)

    total = cpart[0, h]
    for n in range(1, 16):
        sums[n].wait_recv()
        total = total + cin[n]

    zin[z] = total
    for i in (2, 3):
        pl.semaphore_wait(near_sem.at[i], 1)
    zs = []
    for dz in (4, 3, 5, 2, 6, 1, 7):
        copy = pltpu.make_async_remote_copy(
            zin.at[z], zin.at[z], s2_s.at[dz], s2_r.at[dz], device_id=dev(dz=dz), device_id_type=MESH
        )
        copy.start()
        zs.append(copy)
    for copy in zs:
        copy.wait_recv()
    total = zin[0]
    for n in range(1, NZ_RING):
        total = total + zin[n]

    ctot[0, h] = total
    backs = []
    for i in (6, 7, 2, 4, 3, 5, 1, 0):
        dx, dc = STEPS[i]
        for dh in (1, 0):
            if (i, dh) != (0, 0):
                n = i * 2 + dh
                copy = pltpu.make_async_remote_copy(
                    ctot.at[0, h],
                    ctot.at[i, h],
                    s3_s.at[n],
                    s3_r.at[n],
                    device_id=dev(dx=dx, dc=dc, dh=dh),
                    device_id_type=MESH,
                )
                copy.start()
                backs.append(copy)
    for copy in backs:
        copy.wait_recv()

    packed = ctot[...].reshape(8, 16, 128)
    swapped = pltpu.roll(packed.reshape(128, 128), 64, 1).reshape(8, 16, 128)
    corr = jnp.concatenate([packed, swapped], axis=1).reshape(256, 128)
    flat = jnp.transpose(corr)[:64]
    high, low = split(flat)
    for side in (0, 1):
        cts[side, pl.ds(0, 32), :] = high[side * 32 : side * 32 + 32]
        cts[side, pl.ds(32, 32), :] = low[side * 32 : side * 32 + 32]

    def removed(side, out):
        for q0 in range(0, PART, 4):
            at = pl.ds(q0 * NX, 4 * NX)
            both = jnp.dot(cts[side], phi[0, :, at], preferred_element_type=jnp.float32)
            rest = jnp.dot(cts[side, pl.ds(0, 32), :], phi[1, :, at], preferred_element_type=jnp.float32)
            value = both[:32] + both[32:] + rest
            for q in range(4):
                for k in range(NX_RING):
                    out[k, q0 + q] = value[k * 8 : k * 8 + 8, q * NX : (q + 1) * NX]

    removed(1 - yl, rsend)
    order = (2, 1, 3, 0)
    ys = {}
    for dx in order:
        k = (x + dx) % NX_RING
        ys[dx] = pltpu.make_async_remote_copy(
            rsend.at[k], rrecv.at[k], ry_s.at[dx], ry_r.at[dx], device_id=partner, device_id_type=MESH
        )
        ys[dx].start()
    removed(yl, rown)

    own = corr[:32]
    lane = lax.broadcasted_iota(jnp.int32, (ORBS, 128), 1)
    value = own
    for side in (0, 1):
        for k in range(NX_RING):
            source, target = side * 32 + k * 8, k * 16 + side * 8
            if source != target:
                moved = pltpu.roll(own, (target - source) % 128, 1)
                value = jnp.where((lane >= target) & (lane < target + 8), moved, value)
    corr_ref[...] = value[:, :64]

    fins = {}
    for dx in order:
        k = (x + dx) % NX_RING
        ys[dx].wait_recv()
        fin[k] = jnp.swapaxes(rown[k] + rrecv[k], 0, 1)
        for dc in (1, 0):
            source = fin.at[k, pl.ds(((c + dc) % 2) * COLS, COLS)]
            target = rem.at[:, rows_of(me), :]
            n = STEPS.index((dx, dc))
            if n == 0:
                local = pltpu.make_async_copy(source, target, loc_sem.at[3])
                local.start()
            else:
                fins[n] = pltpu.make_async_remote_copy(
                    source, target, fin_s.at[n], fin_r.at[n], device_id=dev(dx=dx, dc=dc), device_id_type=MESH
                )
                fins[n].start()
    local.wait()
    for copy in fins.values():
        copy.wait_recv()
    proj_ref[...] = app[...] - rem[...]

    for group in (hop1, hop2, hop3, orbs.values(), cols.values(), fwds.values(), sums.values(), zs, backs, ys.values(), fins.values()):
        for copy in group:
            copy.wait_send()


def shards(columns, potential, orbitals):
    f32, bf16 = jnp.float32, jnp.bfloat16
    dma = pltpu.SemaphoreType.DMA
    scratch = [
        pltpu.VMEM((COLS, ROWS, NX), f32),
        pltpu.VMEM((ROWS, NX), f32),
        pltpu.VMEM((COLS, ROWS, NX), f32),
        pltpu.VMEM((2, COLS, ROWS, NX), f32),
        pltpu.VMEM((COLS, ROWS, NX), f32),
        pltpu.VMEM((8 * ORBS, PART, NX), f32),
        pltpu.VMEM((2, 8 * ORBS, PART * NX), bf16),
        pltpu.VMEM((64, PART, NX), f32),
        pltpu.VMEM((128, PART * NX), bf16),
        pltpu.VMEM((8, 2, 8, 128), f32),
        pltpu.VMEM((16, 8, 128), f32),
        pltpu.VMEM((NZ_RING, 8, 128), f32),
        pltpu.VMEM((8, 2, 8, 128), f32),
        pltpu.VMEM((2, 64, 256), bf16),
        pltpu.VMEM((NX_RING, PART, 8, NX), f32),
        pltpu.VMEM((NX_RING, PART, 8, NX), f32),
        pltpu.VMEM((NX_RING, PART, 8, NX), f32),
        pltpu.VMEM((NX_RING, 8, PART, NX), f32),
        pltpu.VMEM((COLS, ROWS, NX), f32),
        dma((5,)),
        pltpu.SemaphoreType.REGULAR((4,)),
        dma((8,)), dma((8,)),
        dma((4,)), dma((4,)), dma((4,)), dma((4,)), dma((4,)), dma((4,)),
        dma((8,)), dma((8,)),
        dma((8,)), dma((8,)),
        dma((16,)), dma((16,)),
        dma((8,)), dma((8,)),
        dma((16,)), dma((16,)),
        dma((4,)), dma((4,)),
        dma((8,)), dma((8,)),
    ]
    vmem, anywhere = pl.BlockSpec(memory_space=pltpu.VMEM), pl.BlockSpec(memory_space=pl.ANY)
    projected, correlation = pl.pallas_call(
        kernel,
        out_shape=(
            jax.ShapeDtypeStruct((COLS, ROWS, NX), f32),
            jax.ShapeDtypeStruct((ORBS, 64), f32),
        ),
        in_specs=[anywhere, anywhere, anywhere],
        out_specs=(vmem, vmem),
        scratch_shapes=scratch,
        compiler_params=pltpu.CompilerParams(
            collective_id=0, has_side_effects=True, vmem_limit_bytes=60 * 2**20
        ),
        name="sternheimer",
    )(
        columns.reshape(COLS, ROWS, NX),
        potential.reshape(ROWS, NX),
        orbitals.reshape(ORBS, ROWS, NX),
    )
    return projected.reshape(columns.shape), correlation


def solution(mesh):
    placed = (
        P("band", "space", None, None),
        P("space", None, None),
        P("band", "space", None, None),
    )
    return jax.shard_map(
        shards,
        mesh=mesh,
        in_specs=placed,
        out_specs=(P("band", "space", None, None), P("band", None)),
        check_vma=False,
    )
```

```python
import jax
import jax.numpy as jnp
from jax import lax
from jax.experimental import pallas as pl
from jax.experimental.pallas import tpu as pltpu
from jax.sharding import PartitionSpec as P

COEFFS = (
    -5369.0 / 1800.0,
    12.0 / 7.0,
    -15.0 / 56.0,
    10.0 / 189.0,
    -1.0 / 112.0,
    2.0 / 1925.0,
    -1.0 / 16632.0,
)

MESH = pl.DeviceIdType.MESH
NZ_RING, NX_RING = 8, 4
COLS, ORBS = 4, 32
PLANES, NY, NX = 6, 32, 128
ROWS = PLANES * NY
PART = 16
SPLIT = 8 * PART

STEPS = ((0, 0), (0, 1), (1, 0), (1, 1), (3, 0), (3, 1), (2, 0), (2, 1))
STEPS_Y = ((0, 0), (0, 1), (1, 0), (1, 1))


def kernel(
    col_hbm, pot_hbm, orb_hbm, proj_ref, corr_ref,
    colv, potv, relay, halo, app, phibuf, phi, acol, ahl, cpart, cin, zin, ctot, cts, cts_y,
    rsend, rrecv, rown, fin, ry, ryin, fin_y, rem,
    loc_sem, near_sem, orb_s, orb_r, h1_s, h1_r, h2_s, h2_r, h3_s, h3_r, col_s, col_r, fwd_s, fwd_r,
    orby_s, orby_r, coly_s, coly_r, gat_s, gat_r,
    s1_s, s1_r, s2_s, s2_r, s3_s, s3_r, ry_s, ry_r, fin_s, fin_r, rx_s, rx_r, finy_s, finy_r,
):
    s, b = lax.axis_index("space"), lax.axis_index("band")
    z, h = s // 2, s % 2
    x, yl, c = b // 4, (b // 2) % 2, b % 2
    me = x * 2 + c

    def dev(dz=0, dh=0, dx=0, dy=0, dc=0):
        return (
            ((z + dz) % NZ_RING) * 2 + (h + dh) % 2,
            ((x + dx) % NX_RING) * 4 + ((yl + dy) % 2) * 2 + (c + dc) % 2,
        )

    def part_of(dx, dc):
        return ((x + dx) % NX_RING) * 2 + (c + dc) % 2

    def rows_of(g):
        return pl.ds(pl.multiple_of(g * PART, PART), PART)

    def rows_y(dy, dc):
        g = ((yl + dy) % 2) * 2 + (c + dc) % 2
        return pl.ds(pl.multiple_of(SPLIT + g * PART, PART), PART)

    def slot_of(side, g):
        return pl.ds((side * 8 + g) * COLS, COLS)

    def along_y(step):
        y = (h * 2 + yl + step + 4) % 4
        return y // 2, (z * 2 + y // 2, x * 4 + (y % 2) * 2 + c)

    def signal(sem, to):
        pl.semaphore_signal(sem, inc=1, device_id=to, device_id_type=MESH)

    partner = dev(dy=1)

    barrier = pltpu.get_barrier_semaphore()
    peers = [dev(dx=dx, dc=dc) for dx, dc in STEPS[1:]]
    peers += [along_y(1)[1], along_y(-1)[1], dev(dy=1, dc=1), dev(dz=1), dev(dz=NZ_RING - 1)]
    for peer in peers:
        signal(barrier, peer)

    load_col = pltpu.make_async_copy(col_hbm, colv, loc_sem.at[0])
    load_col.start()
    load_pot = pltpu.make_async_copy(pot_hbm, potv, loc_sem.at[4])
    load_pot.start()
    load_orb = pltpu.make_async_copy(orb_hbm.at[:, rows_of(me), :], phibuf.at[pl.ds(0, ORBS)], loc_sem.at[1])
    load_orb.start()
    load_orb_y = pltpu.make_async_copy(orb_hbm.at[:, rows_y(0, 0), :], phibuf.at[pl.ds(8 * ORBS, ORBS)], loc_sem.at[5])
    load_orb_y.start()

    pl.semaphore_wait(barrier, len(peers))

    signal(near_sem.at[0], dev(dz=1))
    signal(near_sem.at[1], dev(dz=NZ_RING - 1))
    hop1, hop2, hop3 = [], [], []
    for j in (0, 2, 1, 3):
        step = 1 if j < 2 else -1
        h_to, to = along_y(step)
        hop1.append(
            pltpu.make_async_remote_copy(
                col_hbm.at[j], relay.at[j], h1_s.at[j], h1_r.at[j], device_id=to, device_id_type=MESH
            )
        )
        hop2.append(
            pltpu.make_async_remote_copy(
                relay.at[j], halo.at[1 - h_to, j], h2_s.at[j], h2_r.at[j], device_id=to, device_id_type=MESH
            )
        )
        hop3.append(
            pltpu.make_async_remote_copy(
                halo.at[1 - h, j],
                halo.at[h, j],
                h3_s.at[j],
                h3_r.at[j],
                device_id=(((z + 1 - 2 * h + NZ_RING) % NZ_RING) * 2 + h, b),
                device_id_type=MESH,
            )
        )
        hop1[-1].start()

    orbs = {}
    for i, (dx, dc) in enumerate(STEPS):
        if i > 0:
            orbs[i] = pltpu.make_async_remote_copy(
                orb_hbm.at[:, rows_of(part_of(dx, dc)), :],
                phibuf.at[pl.ds(i * ORBS, ORBS)],
                orb_s.at[i],
                orb_r.at[i],
                device_id=dev(dx=dx, dc=dc),
                device_id_type=MESH,
            )
    orbs_y = {}
    for i, (dy, dc) in enumerate(STEPS_Y):
        if i > 0:
            orbs_y[i] = pltpu.make_async_remote_copy(
                orb_hbm.at[:, rows_y(dy, dc), :],
                phibuf.at[pl.ds((8 + i) * ORBS, ORBS)],
                orby_s.at[i],
                orby_r.at[i],
                device_id=dev(dy=dy, dc=dc),
                device_id_type=MESH,
            )
    for i in (2, 4, 3, 5, 1):
        orbs[i].start()
    orbs_y[1].start()
    orbs[6].start()

    load_col.wait()
    load_pot.wait()

    def local_terms(j, carry):
        planes = [colv[j, pl.ds(p * NY, NY), :] for p in range(PLANES)]
        for p in range(PLANES):
            v = planes[p]
            total = (potv[pl.ds(p * NY, NY), :] - 1.5 * COEFFS[0]) * v
            for k in range(1, 7):
                along = pltpu.roll(v, k, 0) + pltpu.roll(v, NY - k, 0)
                along = along + (pltpu.roll(v, k, 1) + pltpu.roll(v, NX - k, 1))
                if p - k >= 0:
                    along = along + planes[p - k]
                if p + k < PLANES:
                    along = along + planes[p + k]
                total = total + (-0.5 * COEFFS[k]) * along
            app[j, pl.ds(p * NY, NY), :] = total
        return carry

    lax.fori_loop(0, COLS, local_terms, 0)

    def split(value):
        high = value.astype(jnp.bfloat16)
        return high, (value - high.astype(jnp.float32)).astype(jnp.bfloat16)

    def lay_out(ref, store, r0, blocks):
        def one(r, carry):
            rows = pl.ds(pl.multiple_of(r0 + r * 16, 16), 16)
            for q0 in range(0, PART, 8):
                high, low = split(jnp.swapaxes(ref[rows, q0 : q0 + 8, :], 0, 1))
                for q in range(8):
                    store(r0 + r * 16, pl.ds((q0 + q) * NX, NX), high[q], low[q])
            return carry

        lax.fori_loop(0, blocks, one, 0)

    def store_orbitals(row, at, high, low):
        rows = pl.ds(pl.multiple_of(row, 16), 16)
        phi[0, rows, at] = high
        phi[1, rows, at] = low

    def columns_to(mode):
        def store(row, at, high, low):
            ahl[mode, pl.ds(pl.multiple_of(row, 16), 16), at] = high
            ahl[mode, pl.ds(pl.multiple_of(64 + row, 16), 16), at] = low

        return store

    for copy, onward in zip(hop1, hop2):
        copy.wait_recv()
        onward.start()
    load_orb.wait()
    orbs[1].wait_recv()
    lay_out(phibuf, store_orbitals, 0, 4)
    load_orb_y.wait()
    orbs_y[1].wait_recv()
    lay_out(phibuf, store_orbitals, 256, 4)
    for copy, onward in zip(hop2, hop3):
        copy.wait_recv()
        onward.start()
    orbs_y[2].start()
    orbs_y[3].start()
    for i in (0, 1):
        pl.semaphore_wait(near_sem.at[i], 1)
    signal(near_sem.at[2], dev(dz=2))
    signal(near_sem.at[3], dev(dz=NZ_RING - 2))

    for copy in hop3:
        copy.wait_recv()

    def halo_terms(j, carry):
        for p in range(PLANES):
            total = app[j, pl.ds(p * NY, NY), :]
            for k in range(1, 7):
                if p - k < 0:
                    total = total + (-0.5 * COEFFS[k]) * halo[0, j, pl.ds((p - k + PLANES) * NY, NY), :]
                if p + k >= PLANES:
                    total = total + (-0.5 * COEFFS[k]) * halo[1, j, pl.ds((p + k - PLANES) * NY, NY), :]
            app[j, pl.ds(p * NY, NY), :] = total
        return carry

    lax.fori_loop(0, COLS, halo_terms, 0)

    own_col = pltpu.make_async_copy(app.at[:, rows_of(me), :], acol.at[0, slot_of(yl, me)], loc_sem.at[2])
    own_col.start()
    own_col_y = pltpu.make_async_copy(app.at[:, rows_y(0, 0), :], acol.at[1, slot_of(yl, me)], loc_sem.at[6])
    own_col_y.start()
    cols, fwds, cols_y, gathers = {}, {}, {}, {}
    for i, (dx, dc) in enumerate(STEPS):
        if i > 0:
            cols[i] = pltpu.make_async_remote_copy(
                app.at[:, rows_of(part_of(dx, dc)), :],
                acol.at[0, slot_of(yl, me)],
                col_s.at[i],
                col_r.at[i],
                device_id=dev(dx=dx, dc=dc),
                device_id_type=MESH,
            )
        came = slot_of(yl, part_of(-dx, -dc))
        fwds[i] = pltpu.make_async_remote_copy(
            app.at[:, rows_of(me), :] if i == 0 else acol.at[0, came],
            acol.at[0, came],
            fwd_s.at[i],
            fwd_r.at[i],
            device_id=partner,
            device_id_type=MESH,
        )
    for i, (dy, dc) in enumerate(STEPS_Y):
        if i > 0:
            cols_y[i] = pltpu.make_async_remote_copy(
                app.at[:, rows_y(dy, dc), :],
                acol.at[1, slot_of(yl, me)],
                coly_s.at[i],
                coly_r.at[i],
                device_id=dev(dy=dy, dc=dc),
                device_id_type=MESH,
            )
    for dx in (2, 1, 3):
        for dy in (0, 1):
            block = acol.at[1, pl.ds(((yl + dy) % 2) * 32 + x * 8, 8)]
            gathers[dx * 2 + dy] = pltpu.make_async_remote_copy(
                block, block, gat_s.at[dx * 2 + dy], gat_r.at[dx * 2 + dy], device_id=dev(dx=dx), device_id_type=MESH
            )
    for i in (6, 7, 2, 4, 3, 5, 1):
        cols[i].start()
    for i in (2, 3, 1):
        cols_y[i].start()
    fwds[0].start()
    orbs[7].start()
    own_col_y.wait()
    cols_y[1].wait_recv()
    for dx in (2, 1, 3):
        gathers[dx * 2].start()
    for i in (1, 2, 4, 3, 5):
        cols[i].wait_recv()
        fwds[i].start()
    for i in (2, 3):
        cols_y[i].wait_recv()
    for dx in (2, 1, 3):
        gathers[dx * 2 + 1].start()
    for i in (6, 7):
        cols[i].wait_recv()
        fwds[i].start()

    for i in (2, 3, 4, 5):
        orbs[i].wait_recv()
    lay_out(phibuf, store_orbitals, 64, 8)
    for i in (2, 3):
        orbs_y[i].wait_recv()
    lay_out(phibuf, store_orbitals, 320, 4)

    own_col.wait()
    for i in range(8):
        fwds[i].wait_recv()
    lay_out(acol.at[0], columns_to(0), 0, 4)

    half_lanes = lax.broadcasted_iota(jnp.int32, (16, 128), 1) < 64
    dims = (((1,), (1,)), ((), ()))

    def correlate(mode, i0, n):
        rows = pl.ds(i0 * ORBS, n * ORBS)
        high = lax.dot_general(phi[0, rows, :], ahl[mode], dims, preferred_element_type=jnp.float32)
        low = lax.dot_general(phi[1, rows, :], ahl[mode], dims, preferred_element_type=jnp.float32)
        value = high + pltpu.roll(high, 64, 1) + low
        for i in range(n):
            first = value[i * ORBS : i * ORBS + 16]
            second = value[i * ORBS + 16 : i * ORBS + 32]
            packed = jnp.where(half_lanes, first, pltpu.roll(second, 64, 1))
            if i0 + i in (8, 9):
                cpart[i0 + i - 8, 0] += packed[:8]
                cpart[i0 + i - 8, 1] += packed[8:]
            else:
                cpart[i0 + i, 0] = packed[:8]
                cpart[i0 + i, 1] = packed[8:]

    sums = {}

    def send_parts(i):
        if i < 8:
            dx, dc = STEPS[i]
            dy, n0 = 0, i * 2
        else:
            dx, (dy, dc) = 0, STEPS_Y[i - 8]
            n0 = i * 2 - 4
        for dh in (0, 1):
            if (i, dh) != (0, 0):
                n = n0 + dh
                sums[n] = pltpu.make_async_remote_copy(
                    cpart.at[i, (h + dh) % 2],
                    cin.at[n],
                    s1_s.at[n],
                    s1_r.at[n],
                    device_id=dev(dx=-dx, dy=dy, dc=-dc, dh=dh),
                    device_id_type=MESH,
                )
                sums[n].start()

    correlate(0, 0, 6)
    for i in (2, 4, 3, 5):
        send_parts(i)
    for copy in gathers.values():
        copy.wait_recv()
    lay_out(acol.at[1], columns_to(1), 0, 4)
    correlate(1, 8, 4)
    for i in (10, 11, 1, 0):
        send_parts(i)
    for i in (6, 7):
        orbs[i].wait_recv()
    lay_out(phibuf, store_orbitals, 192, 4)
    correlate(0, 6, 2)
    send_parts(6)
    send_parts(7)

    total = cpart[0, h]
    for n in range(1, 20):
        sums[n].wait_recv()
        total = total + cin[n]

    zin[z] = total
    for i in (2, 3):
        pl.semaphore_wait(near_sem.at[i], 1)
    zs = []
    for dz in (4, 3, 5, 2, 6, 1, 7):
        copy = pltpu.make_async_remote_copy(
            zin.at[z], zin.at[z], s2_s.at[dz], s2_r.at[dz], device_id=dev(dz=dz), device_id_type=MESH
        )
        copy.start()
        zs.append(copy)
    for copy in zs:
        copy.wait_recv()
    total = zin[0]
    for n in range(1, NZ_RING):
        total = total + zin[n]

    ctot[0, h] = total
    backs = []
    users = [(i, dx, 0, dc) for i, (dx, dc) in enumerate(STEPS)]
    users += [(8, 0, 1, 0), (9, 0, 1, 1)]
    for i in (6, 7, 8, 9, 2, 4, 3, 5, 1, 0):
        _, dx, dy, dc = users[i]
        for dh in (1, 0):
            if (i, dh) != (0, 0):
                n = i * 2 + dh
                copy = pltpu.make_async_remote_copy(
                    ctot.at[0, h],
                    ctot.at[i, h],
                    s3_s.at[n],
                    s3_r.at[n],
                    device_id=dev(dx=dx, dy=dy, dc=dc, dh=dh),
                    device_id_type=MESH,
                )
                copy.start()
                backs.append(copy)
    for copy in backs:
        copy.wait_recv()

    packed = ctot[...].reshape(10, 16, 128)
    swapped = pltpu.roll(packed.reshape(160, 128), 64, 1).reshape(10, 16, 128)
    corr = jnp.concatenate([packed, swapped], axis=1).reshape(320, 128)
    corr_y = jnp.concatenate([corr[:64], corr[256:]], axis=0)

    def operands(value, out):
        high, low = split(jnp.transpose(value)[:64])
        for side in (0, 1):
            out[side, pl.ds(0, 32), :] = high[side * 32 : side * 32 + 32]
            out[side, pl.ds(32, 32), :] = low[side * 32 : side * 32 + 32]

    operands(corr[:256], cts)

    def removed(left, rows, side, out):
        for q0 in range(0, PART, 4):
            at = pl.ds(q0 * NX, 4 * NX)
            both = jnp.dot(left[side], phi[0, rows, at], preferred_element_type=jnp.float32)
            rest = jnp.dot(left[side, pl.ds(0, 32), :], phi[1, rows, at], preferred_element_type=jnp.float32)
            value = both[:32] + both[32:] + rest
            for q in range(4):
                for k in range(NX_RING):
                    out(k, q0 + q, value[k * 8 : k * 8 + 8, q * NX : (q + 1) * NX])

    def to_send(k, q, value):
        rsend[k, q] = value

    def to_own(k, q, value):
        rown[k, q] = value

    first, last = pl.ds(0, 256), pl.ds(256, 128)
    removed(cts, first, 1 - yl, to_send)
    order = (2, 1, 3, 0)
    ys = {}
    for dx in order:
        k = (x + dx) % NX_RING
        ys[dx] = pltpu.make_async_remote_copy(
            rsend.at[k], rrecv.at[k], ry_s.at[dx], ry_r.at[dx], device_id=partner, device_id_type=MESH
        )
        ys[dx].start()
    operands(corr_y, cts_y)
    for side in (0, 1):

        def to_x(k, q, value):
            ry[k, side, q] = value

        removed(cts_y, last, side, to_x)
    xs = {}
    for dx in (2, 1, 3):
        xs[dx] = pltpu.make_async_remote_copy(
            ry.at[(x + dx) % NX_RING], ryin.at[dx], rx_s.at[dx], rx_r.at[dx], device_id=dev(dx=dx), device_id_type=MESH
        )
        xs[dx].start()
    removed(cts, first, yl, to_own)

    own = corr[:32]
    lane = lax.broadcasted_iota(jnp.int32, (ORBS, 128), 1)
    value = own
    for side in (0, 1):
        for k in range(NX_RING):
            source, target = side * 32 + k * 8, k * 16 + side * 8
            if source != target:
                moved = pltpu.roll(own, (target - source) % 128, 1)
                value = jnp.where((lane >= target) & (lane < target + 8), moved, value)
    corr_ref[...] = value[:, :64]

    fins = {}
    for dx in order:
        k = (x + dx) % NX_RING
        ys[dx].wait_recv()
        fin[k] = jnp.swapaxes(rown[k] + rrecv[k], 0, 1)
        for dc in (1, 0):
            source = fin.at[k, pl.ds(((c + dc) % 2) * COLS, COLS)]
            target = rem.at[:, rows_of(me), :]
            n = STEPS.index((dx, dc))
            if n == 0:
                local = pltpu.make_async_copy(source, target, loc_sem.at[3])
                local.start()
            else:
                fins[n] = pltpu.make_async_remote_copy(
                    source, target, fin_s.at[n], fin_r.at[n], device_id=dev(dx=dx, dc=dc), device_id_type=MESH
                )
                fins[n].start()
    value = ry[x]
    for dx in (1, 3, 2):
        xs[dx].wait_recv()
        value = value + ryin[dx]
    for side in (0, 1):
        fin_y[side] = jnp.swapaxes(value[side], 0, 1)
    for i in (2, 3, 1, 0):
        dy, dc = STEPS_Y[i]
        source = fin_y.at[(yl + dy) % 2, pl.ds(((c + dc) % 2) * COLS, COLS)]
        target = rem.at[:, rows_y(0, 0), :]
        if i == 0:
            local_y = pltpu.make_async_copy(source, target, loc_sem.at[7])
            local_y.start()
        else:
            fins[8 + i] = pltpu.make_async_remote_copy(
                source, target, finy_s.at[i], finy_r.at[i], device_id=dev(dy=dy, dc=dc), device_id_type=MESH
            )
            fins[8 + i].start()
    local.wait()
    local_y.wait()
    for copy in fins.values():
        copy.wait_recv()
    proj_ref[...] = app[...] - rem[...]

    groups = [hop1, hop2, hop3, zs, backs]
    groups += [g.values() for g in (orbs, orbs_y, cols, fwds, cols_y, gathers, sums, ys, xs, fins)]
    for group in groups:
        for copy in group:
            copy.wait_send()


def shards(columns, potential, orbitals):
    f32, bf16 = jnp.float32, jnp.bfloat16
    dma = pltpu.SemaphoreType.DMA
    scratch = [
        pltpu.VMEM((COLS, ROWS, NX), f32),
        pltpu.VMEM((ROWS, NX), f32),
        pltpu.VMEM((COLS, ROWS, NX), f32),
        pltpu.VMEM((2, COLS, ROWS, NX), f32),
        pltpu.VMEM((COLS, ROWS, NX), f32),
        pltpu.VMEM((12 * ORBS, PART, NX), f32),
        pltpu.VMEM((2, 12 * ORBS, PART * NX), bf16),
        pltpu.VMEM((2, 64, PART, NX), f32),
        pltpu.VMEM((2, 128, PART * NX), bf16),
        pltpu.VMEM((12, 2, 8, 128), f32),
        pltpu.VMEM((20, 8, 128), f32),
        pltpu.VMEM((NZ_RING, 8, 128), f32),
        pltpu.VMEM((10, 2, 8, 128), f32),
        pltpu.VMEM((2, 64, 256), bf16),
        pltpu.VMEM((2, 64, 128), bf16),
        pltpu.VMEM((NX_RING, PART, 8, NX), f32),
        pltpu.VMEM((NX_RING, PART, 8, NX), f32),
        pltpu.VMEM((NX_RING, PART, 8, NX), f32),
        pltpu.VMEM((NX_RING, 8, PART, NX), f32),
        pltpu.VMEM((NX_RING, 2, PART, 8, NX), f32),
        pltpu.VMEM((NX_RING, 2, PART, 8, NX), f32),
        pltpu.VMEM((2, 8, PART, NX), f32),
        pltpu.VMEM((COLS, ROWS, NX), f32),
        dma((8,)),
        pltpu.SemaphoreType.REGULAR((4,)),
        dma((8,)), dma((8,)),
        dma((4,)), dma((4,)), dma((4,)), dma((4,)), dma((4,)), dma((4,)),
        dma((8,)), dma((8,)),
        dma((8,)), dma((8,)),
        dma((4,)), dma((4,)),
        dma((4,)), dma((4,)),
        dma((8,)), dma((8,)),
        dma((20,)), dma((20,)),
        dma((8,)), dma((8,)),
        dma((20,)), dma((20,)),
        dma((4,)), dma((4,)),
        dma((8,)), dma((8,)),
        dma((4,)), dma((4,)),
        dma((4,)), dma((4,)),
    ]
    vmem, anywhere = pl.BlockSpec(memory_space=pltpu.VMEM), pl.BlockSpec(memory_space=pl.ANY)
    projected, correlation = pl.pallas_call(
        kernel,
        out_shape=(
            jax.ShapeDtypeStruct((COLS, ROWS, NX), f32),
            jax.ShapeDtypeStruct((ORBS, 64), f32),
        ),
        in_specs=[anywhere, anywhere, anywhere],
        out_specs=(vmem, vmem),
        scratch_shapes=scratch,
        compiler_params=pltpu.CompilerParams(
            collective_id=0, has_side_effects=True, vmem_limit_bytes=60 * 2**20
        ),
        name="sternheimer",
    )(
        columns.reshape(COLS, ROWS, NX),
        potential.reshape(ROWS, NX),
        orbitals.reshape(ORBS, ROWS, NX),
    )
    return projected.reshape(columns.shape), correlation


def solution(mesh):
    placed = (
        P("band", "space", None, None),
        P("space", None, None),
        P("band", "space", None, None),
    )
    return jax.shard_map(
        shards,
        mesh=mesh,
        in_specs=placed,
        out_specs=(P("band", "space", None, None), P("band", None)),
        check_vma=False,
    )
```

```python
import jax
import jax.numpy as jnp
from jax import lax
from jax.experimental import pallas as pl
from jax.experimental.pallas import tpu as pltpu
from jax.sharding import PartitionSpec as P

COEFFS = (
    -5369.0 / 1800.0,
    12.0 / 7.0,
    -15.0 / 56.0,
    10.0 / 189.0,
    -1.0 / 112.0,
    2.0 / 1925.0,
    -1.0 / 16632.0,
)

MESH = pl.DeviceIdType.MESH
NZ_RING, NX_RING = 8, 4
COLS, ORBS = 4, 32
PLANES, NY, NX = 6, 32, 128
ROWS = PLANES * NY
PART = 16
SPLIT = 8 * PART

STEPS = ((0, 0), (0, 1), (1, 0), (1, 1), (3, 0), (3, 1), (2, 0), (2, 1))
STEPS_Y = ((0, 0), (0, 1), (1, 0), (1, 1))


def kernel(
    col_hbm, pot_hbm, orb_hbm, proj_ref, corr_ref,
    colv, potv, halo, app, phibuf, phi, acol, ahl, cpart, cin, zin, ctot, cts, cts_y,
    rsend, rrecv, rown, fin, ry, ryin, fin_y, rem,
    loc_sem, near_sem, orb_s, orb_r, h_s, h_r, col_s, col_r, fwd_s, fwd_r,
    orby_s, orby_r, coly_s, coly_r, gat_s, gat_r,
    s1_s, s1_r, s2_s, s2_r, s3_s, s3_r, ry_s, ry_r, fin_s, fin_r, rx_s, rx_r, finy_s, finy_r,
):
    s, b = lax.axis_index("space"), lax.axis_index("band")
    z, h = s // 2, s % 2
    x, yl, c = b // 4, (b // 2) % 2, b % 2
    me = x * 2 + c

    def dev(dz=0, dh=0, dx=0, dy=0, dc=0):
        return (
            ((z + dz) % NZ_RING) * 2 + (h + dh) % 2,
            ((x + dx) % NX_RING) * 4 + ((yl + dy) % 2) * 2 + (c + dc) % 2,
        )

    def part_of(dx, dc):
        return ((x + dx) % NX_RING) * 2 + (c + dc) % 2

    def rows_of(g):
        return pl.ds(pl.multiple_of(g * PART, PART), PART)

    def rows_y(dy, dc):
        g = ((yl + dy) % 2) * 2 + (c + dc) % 2
        return pl.ds(pl.multiple_of(SPLIT + g * PART, PART), PART)

    def slot_of(side, g):
        return pl.ds((side * 8 + g) * COLS, COLS)

    def signal(sem, to):
        pl.semaphore_signal(sem, inc=1, device_id=to, device_id_type=MESH)

    partner = dev(dy=1)
    same_z, other_z = dev(dh=1), (((s + 16 + 2 * h - 1) % 16), b)

    barrier = pltpu.get_barrier_semaphore()
    peers = [dev(dx=dx, dc=dc) for dx, dc in STEPS[1:]]
    peers += [partner, dev(dy=1, dc=1), same_z, other_z, dev(dz=1), dev(dz=NZ_RING - 1)]
    for peer in peers:
        signal(barrier, peer)

    load_col = pltpu.make_async_copy(col_hbm, colv, loc_sem.at[0])
    load_col.start()
    load_pot = pltpu.make_async_copy(pot_hbm, potv, loc_sem.at[4])
    load_pot.start()
    load_orb = pltpu.make_async_copy(orb_hbm.at[:, rows_of(me), :], phibuf.at[pl.ds(0, ORBS)], loc_sem.at[1])
    load_orb.start()
    load_orb_y = pltpu.make_async_copy(orb_hbm.at[:, rows_y(0, 0), :], phibuf.at[pl.ds(8 * ORBS, ORBS)], loc_sem.at[5])
    load_orb_y.start()

    pl.semaphore_wait(barrier, len(peers))

    signal(near_sem.at[0], dev(dz=1))
    signal(near_sem.at[1], dev(dz=NZ_RING - 1))

    def halo_copy(j, source, side, sem, to):
        return pltpu.make_async_remote_copy(
            source, halo.at[side, j], h_s.at[sem], h_r.at[sem], device_id=to, device_id_type=MESH
        )

    to_same = [halo_copy(j, col_hbm.at[j], h, j, same_z) for j in range(COLS)]
    to_other = [halo_copy(j, col_hbm.at[j], 1 - h, 4 + j, other_z) for j in range(2)]
    beside = ((z + 1 - 2 * h + NZ_RING) % NZ_RING) * 2 + h, b
    onward = [halo_copy(j, halo.at[1 - h, j], h, 4 + j, beside) for j in range(2, COLS)]
    for copy in (to_same[2], to_same[3], to_other[0], to_same[0], to_other[1], to_same[1]):
        copy.start()

    orbs = {}
    for i, (dx, dc) in enumerate(STEPS):
        if i > 0:
            orbs[i] = pltpu.make_async_remote_copy(
                orb_hbm.at[:, rows_of(part_of(dx, dc)), :],
                phibuf.at[pl.ds(i * ORBS, ORBS)],
                orb_s.at[i],
                orb_r.at[i],
                device_id=dev(dx=dx, dc=dc),
                device_id_type=MESH,
            )
    orbs_y = {}
    for i, (dy, dc) in enumerate(STEPS_Y):
        if i > 0:
            orbs_y[i] = pltpu.make_async_remote_copy(
                orb_hbm.at[:, rows_y(dy, dc), :],
                phibuf.at[pl.ds((8 + i) * ORBS, ORBS)],
                orby_s.at[i],
                orby_r.at[i],
                device_id=dev(dy=dy, dc=dc),
                device_id_type=MESH,
            )
    for i in (2, 4, 3, 5, 1):
        orbs[i].start()
    orbs_y[1].start()
    orbs[6].start()

    load_col.wait()
    load_pot.wait()

    def local_terms(j, carry):
        planes = [colv[j, pl.ds(p * NY, NY), :] for p in range(PLANES)]
        for p in range(PLANES):
            v = planes[p]
            total = (potv[pl.ds(p * NY, NY), :] - 1.5 * COEFFS[0]) * v
            for k in range(1, 7):
                along = pltpu.roll(v, k, 0) + pltpu.roll(v, NY - k, 0)
                along = along + (pltpu.roll(v, k, 1) + pltpu.roll(v, NX - k, 1))
                if p - k >= 0:
                    along = along + planes[p - k]
                if p + k < PLANES:
                    along = along + planes[p + k]
                total = total + (-0.5 * COEFFS[k]) * along
            app[j, pl.ds(p * NY, NY), :] = total
        return carry

    lax.fori_loop(0, COLS, local_terms, 0)
    for copy, follower in zip(to_same[2:], onward):
        copy.wait_recv()
        follower.start()

    def split(value):
        high = value.astype(jnp.bfloat16)
        return high, (value - high.astype(jnp.float32)).astype(jnp.bfloat16)

    def lay_out(ref, store, r0, blocks):
        def one(r, carry):
            rows = pl.ds(pl.multiple_of(r0 + r * 16, 16), 16)
            for q0 in range(0, PART, 8):
                high, low = split(jnp.swapaxes(ref[rows, q0 : q0 + 8, :], 0, 1))
                for q in range(8):
                    store(r0 + r * 16, pl.ds((q0 + q) * NX, NX), high[q], low[q])
            return carry

        lax.fori_loop(0, blocks, one, 0)

    def store_orbitals(row, at, high, low):
        rows = pl.ds(pl.multiple_of(row, 16), 16)
        phi[0, rows, at] = high
        phi[1, rows, at] = low

    def columns_to(mode):
        def store(row, at, high, low):
            ahl[mode, pl.ds(pl.multiple_of(row, 16), 16), at] = high
            ahl[mode, pl.ds(pl.multiple_of(64 + row, 16), 16), at] = low

        return store

    orbs_y[2].start()
    orbs_y[3].start()
    load_orb.wait()
    orbs[1].wait_recv()
    lay_out(phibuf, store_orbitals, 0, 4)
    load_orb_y.wait()
    orbs_y[1].wait_recv()
    lay_out(phibuf, store_orbitals, 256, 4)
    for i in (0, 1):
        pl.semaphore_wait(near_sem.at[i], 1)
    signal(near_sem.at[2], dev(dz=2))
    signal(near_sem.at[3], dev(dz=NZ_RING - 2))

    for copy in (*onward, *to_same[:2], *to_other):
        copy.wait_recv()

    def halo_terms(j, carry):
        for p in range(PLANES):
            total = app[j, pl.ds(p * NY, NY), :]
            for k in range(1, 7):
                if p - k < 0:
                    total = total + (-0.5 * COEFFS[k]) * halo[0, j, pl.ds((p - k + PLANES) * NY, NY), :]
                if p + k >= PLANES:
                    total = total + (-0.5 * COEFFS[k]) * halo[1, j, pl.ds((p + k - PLANES) * NY, NY), :]
            app[j, pl.ds(p * NY, NY), :] = total
        return carry

    lax.fori_loop(0, COLS, halo_terms, 0)

    own_col = pltpu.make_async_copy(app.at[:, rows_of(me), :], acol.at[0, slot_of(yl, me)], loc_sem.at[2])
    own_col.start()
    own_col_y = pltpu.make_async_copy(app.at[:, rows_y(0, 0), :], acol.at[1, slot_of(yl, me)], loc_sem.at[6])
    own_col_y.start()
    cols, fwds, cols_y, gathers = {}, {}, {}, {}
    for i, (dx, dc) in enumerate(STEPS):
        if i > 0:
            cols[i] = pltpu.make_async_remote_copy(
                app.at[:, rows_of(part_of(dx, dc)), :],
                acol.at[0, slot_of(yl, me)],
                col_s.at[i],
                col_r.at[i],
                device_id=dev(dx=dx, dc=dc),
                device_id_type=MESH,
            )
        came = slot_of(yl, part_of(-dx, -dc))
        fwds[i] = pltpu.make_async_remote_copy(
            app.at[:, rows_of(me), :] if i == 0 else acol.at[0, came],
            acol.at[0, came],
            fwd_s.at[i],
            fwd_r.at[i],
            device_id=partner,
            device_id_type=MESH,
        )
    for i, (dy, dc) in enumerate(STEPS_Y):
        if i > 0:
            cols_y[i] = pltpu.make_async_remote_copy(
                app.at[:, rows_y(dy, dc), :],
                acol.at[1, slot_of(yl, me)],
                coly_s.at[i],
                coly_r.at[i],
                device_id=dev(dy=dy, dc=dc),
                device_id_type=MESH,
            )
    for dx in (2, 1, 3):
        for dy in (0, 1):
            block = acol.at[1, pl.ds(((yl + dy) % 2) * 32 + x * 8, 8)]
            gathers[dx * 2 + dy] = pltpu.make_async_remote_copy(
                block, block, gat_s.at[dx * 2 + dy], gat_r.at[dx * 2 + dy], device_id=dev(dx=dx), device_id_type=MESH
            )
    for i in (6, 7, 2, 4, 3, 5, 1):
        cols[i].start()
    for i in (2, 3, 1):
        cols_y[i].start()
    fwds[0].start()
    orbs[7].start()
    own_col_y.wait()
    cols_y[1].wait_recv()
    for dx in (2, 1, 3):
        gathers[dx * 2].start()
    for i in (1, 2, 4, 3, 5):
        cols[i].wait_recv()
        fwds[i].start()
    for i in (2, 3):
        cols_y[i].wait_recv()
    for dx in (2, 1, 3):
        gathers[dx * 2 + 1].start()
    for i in (6, 7):
        cols[i].wait_recv()
        fwds[i].start()

    for i in (2, 3, 4, 5, 6, 7):
        orbs[i].wait_recv()
    lay_out(phibuf, store_orbitals, 64, 12)
    for i in (2, 3):
        orbs_y[i].wait_recv()
    lay_out(phibuf, store_orbitals, 320, 4)

    own_col.wait()
    for i in range(8):
        fwds[i].wait_recv()
    lay_out(acol.at[0], columns_to(0), 0, 4)

    half_lanes = lax.broadcasted_iota(jnp.int32, (16, 128), 1) < 64
    dims = (((1,), (1,)), ((), ()))

    def correlate(mode, i0, n):
        rows = pl.ds(i0 * ORBS, n * ORBS)
        high = lax.dot_general(phi[0, rows, :], ahl[mode], dims, preferred_element_type=jnp.float32)
        low = lax.dot_general(phi[1, rows, :], ahl[mode], dims, preferred_element_type=jnp.float32)
        value = high + pltpu.roll(high, 64, 1) + low
        for i in range(n):
            first = value[i * ORBS : i * ORBS + 16]
            second = value[i * ORBS + 16 : i * ORBS + 32]
            packed = jnp.where(half_lanes, first, pltpu.roll(second, 64, 1))
            if i0 + i in (8, 9):
                cpart[i0 + i - 8, 0] += packed[:8]
                cpart[i0 + i - 8, 1] += packed[8:]
            else:
                cpart[i0 + i, 0] = packed[:8]
                cpart[i0 + i, 1] = packed[8:]

    sums = {}

    def send_parts(i):
        if i < 8:
            dx, dc = STEPS[i]
            dy, n0 = 0, i * 2
        else:
            dx, (dy, dc) = 0, STEPS_Y[i - 8]
            n0 = i * 2 - 4
        for dh in (0, 1):
            if (i, dh) != (0, 0):
                n = n0 + dh
                sums[n] = pltpu.make_async_remote_copy(
                    cpart.at[i, (h + dh) % 2],
                    cin.at[n],
                    s1_s.at[n],
                    s1_r.at[n],
                    device_id=dev(dx=-dx, dy=dy, dc=-dc, dh=dh),
                    device_id_type=MESH,
                )
                sums[n].start()

    correlate(0, 0, 8)
    for i in (6, 7, 2, 4, 3, 5):
        send_parts(i)
    for copy in gathers.values():
        copy.wait_recv()
    lay_out(acol.at[1], columns_to(1), 0, 4)
    correlate(1, 8, 4)
    for i in (10, 11, 1, 0):
        send_parts(i)

    total = cpart[0, h]
    for n in range(1, 20):
        sums[n].wait_recv()
        total = total + cin[n]

    zin[z] = total
    for i in (2, 3):
        pl.semaphore_wait(near_sem.at[i], 1)
    zs = []
    for dz in (4, 3, 5, 2, 6, 1, 7):
        copy = pltpu.make_async_remote_copy(
            zin.at[z], zin.at[z], s2_s.at[dz], s2_r.at[dz], device_id=dev(dz=dz), device_id_type=MESH
        )
        copy.start()
        zs.append(copy)
    for copy in zs:
        copy.wait_recv()
    total = zin[0]
    for n in range(1, NZ_RING):
        total = total + zin[n]

    ctot[0, h] = total
    backs = []
    users = [(i, dx, 0, dc) for i, (dx, dc) in enumerate(STEPS)]
    users += [(8, 0, 1, 0), (9, 0, 1, 1)]
    for i in (6, 7, 8, 9, 2, 4, 3, 5, 1, 0):
        _, dx, dy, dc = users[i]
        for dh in (1, 0):
            if (i, dh) != (0, 0):
                n = i * 2 + dh
                copy = pltpu.make_async_remote_copy(
                    ctot.at[0, h],
                    ctot.at[i, h],
                    s3_s.at[n],
                    s3_r.at[n],
                    device_id=dev(dx=dx, dy=dy, dc=dc, dh=dh),
                    device_id_type=MESH,
                )
                copy.start()
                backs.append(copy)
    for copy in backs:
        copy.wait_recv()

    packed = ctot[...].reshape(10, 16, 128)
    swapped = pltpu.roll(packed.reshape(160, 128), 64, 1).reshape(10, 16, 128)
    corr = jnp.concatenate([packed, swapped], axis=1).reshape(320, 128)
    corr_y = jnp.concatenate([corr[:64], corr[256:]], axis=0)

    def operands(value, out):
        high, low = split(jnp.transpose(value)[:64])
        for side in (0, 1):
            out[side, pl.ds(0, 32), :] = high[side * 32 : side * 32 + 32]
            out[side, pl.ds(32, 32), :] = low[side * 32 : side * 32 + 32]

    def removed(left, rows, side, out):
        for q0 in range(0, PART, 4):
            at = pl.ds(q0 * NX, 4 * NX)
            both = jnp.dot(left[side], phi[0, rows, at], preferred_element_type=jnp.float32)
            rest = jnp.dot(left[side, pl.ds(0, 32), :], phi[1, rows, at], preferred_element_type=jnp.float32)
            value = both[:32] + both[32:] + rest
            for q in range(4):
                for k in range(NX_RING):
                    out(k, q0 + q, value[k * 8 : k * 8 + 8, q * NX : (q + 1) * NX])

    def to_send(k, q, value):
        rsend[k, q] = value

    def to_own(k, q, value):
        rown[k, q] = value

    first, last = pl.ds(0, 256), pl.ds(256, 128)
    operands(corr_y, cts_y)
    for side in (0, 1):

        def to_x(k, q, value):
            ry[k, side, q] = value

        removed(cts_y, last, side, to_x)
    xs = {}
    for dx in (2, 1, 3):
        xs[dx] = pltpu.make_async_remote_copy(
            ry.at[(x + dx) % NX_RING], ryin.at[dx], rx_s.at[dx], rx_r.at[dx], device_id=dev(dx=dx), device_id_type=MESH
        )
        xs[dx].start()
    operands(corr[:256], cts)
    removed(cts, first, 1 - yl, to_send)
    order = (2, 1, 3, 0)
    ys = {}
    for dx in order:
        k = (x + dx) % NX_RING
        ys[dx] = pltpu.make_async_remote_copy(
            rsend.at[k], rrecv.at[k], ry_s.at[dx], ry_r.at[dx], device_id=partner, device_id_type=MESH
        )
        ys[dx].start()
    removed(cts, first, yl, to_own)

    own = corr[:32]
    lane = lax.broadcasted_iota(jnp.int32, (ORBS, 128), 1)
    value = own
    for side in (0, 1):
        for k in range(NX_RING):
            source, target = side * 32 + k * 8, k * 16 + side * 8
            if source != target:
                moved = pltpu.roll(own, (target - source) % 128, 1)
                value = jnp.where((lane >= target) & (lane < target + 8), moved, value)
    corr_ref[...] = value[:, :64]

    fins = {}
    for dx in order:
        k = (x + dx) % NX_RING
        ys[dx].wait_recv()
        fin[k] = jnp.swapaxes(rown[k] + rrecv[k], 0, 1)
        for dc in (1, 0):
            source = fin.at[k, pl.ds(((c + dc) % 2) * COLS, COLS)]
            target = rem.at[:, rows_of(me), :]
            n = STEPS.index((dx, dc))
            if n == 0:
                local = pltpu.make_async_copy(source, target, loc_sem.at[3])
                local.start()
            else:
                fins[n] = pltpu.make_async_remote_copy(
                    source, target, fin_s.at[n], fin_r.at[n], device_id=dev(dx=dx, dc=dc), device_id_type=MESH
                )
                fins[n].start()
    value = ry[x]
    for dx in (1, 3, 2):
        xs[dx].wait_recv()
        value = value + ryin[dx]
    for side in (0, 1):
        fin_y[side] = jnp.swapaxes(value[side], 0, 1)
    for i in (2, 3, 1, 0):
        dy, dc = STEPS_Y[i]
        source = fin_y.at[(yl + dy) % 2, pl.ds(((c + dc) % 2) * COLS, COLS)]
        target = rem.at[:, rows_y(0, 0), :]
        if i == 0:
            local_y = pltpu.make_async_copy(source, target, loc_sem.at[7])
            local_y.start()
        else:
            fins[8 + i] = pltpu.make_async_remote_copy(
                source, target, finy_s.at[i], finy_r.at[i], device_id=dev(dy=dy, dc=dc), device_id_type=MESH
            )
            fins[8 + i].start()
    local.wait()
    local_y.wait()
    for copy in fins.values():
        copy.wait_recv()
    proj_ref[...] = app[...] - rem[...]

    groups = [to_same, to_other, onward, zs, backs]
    groups += [g.values() for g in (orbs, orbs_y, cols, fwds, cols_y, gathers, sums, ys, xs, fins)]
    for group in groups:
        for copy in group:
            copy.wait_send()


def shards(columns, potential, orbitals):
    f32, bf16 = jnp.float32, jnp.bfloat16
    dma = pltpu.SemaphoreType.DMA
    scratch = [
        pltpu.VMEM((COLS, ROWS, NX), f32),
        pltpu.VMEM((ROWS, NX), f32),
        pltpu.VMEM((2, COLS, ROWS, NX), f32),
        pltpu.VMEM((COLS, ROWS, NX), f32),
        pltpu.VMEM((12 * ORBS, PART, NX), f32),
        pltpu.VMEM((2, 12 * ORBS, PART * NX), bf16),
        pltpu.VMEM((2, 64, PART, NX), f32),
        pltpu.VMEM((2, 128, PART * NX), bf16),
        pltpu.VMEM((12, 2, 8, 128), f32),
        pltpu.VMEM((20, 8, 128), f32),
        pltpu.VMEM((NZ_RING, 8, 128), f32),
        pltpu.VMEM((10, 2, 8, 128), f32),
        pltpu.VMEM((2, 64, 256), bf16),
        pltpu.VMEM((2, 64, 128), bf16),
        pltpu.VMEM((NX_RING, PART, 8, NX), f32),
        pltpu.VMEM((NX_RING, PART, 8, NX), f32),
        pltpu.VMEM((NX_RING, PART, 8, NX), f32),
        pltpu.VMEM((NX_RING, 8, PART, NX), f32),
        pltpu.VMEM((NX_RING, 2, PART, 8, NX), f32),
        pltpu.VMEM((NX_RING, 2, PART, 8, NX), f32),
        pltpu.VMEM((2, 8, PART, NX), f32),
        pltpu.VMEM((COLS, ROWS, NX), f32),
        dma((8,)),
        pltpu.SemaphoreType.REGULAR((4,)),
        dma((8,)), dma((8,)),
        dma((8,)), dma((8,)),
        dma((8,)), dma((8,)),
        dma((8,)), dma((8,)),
        dma((4,)), dma((4,)),
        dma((4,)), dma((4,)),
        dma((8,)), dma((8,)),
        dma((20,)), dma((20,)),
        dma((8,)), dma((8,)),
        dma((20,)), dma((20,)),
        dma((4,)), dma((4,)),
        dma((8,)), dma((8,)),
        dma((4,)), dma((4,)),
        dma((4,)), dma((4,)),
    ]
    vmem, anywhere = pl.BlockSpec(memory_space=pltpu.VMEM), pl.BlockSpec(memory_space=pl.ANY)
    projected, correlation = pl.pallas_call(
        kernel,
        out_shape=(
            jax.ShapeDtypeStruct((COLS, ROWS, NX), f32),
            jax.ShapeDtypeStruct((ORBS, 64), f32),
        ),
        in_specs=[anywhere, anywhere, anywhere],
        out_specs=(vmem, vmem),
        scratch_shapes=scratch,
        compiler_params=pltpu.CompilerParams(
            collective_id=0, has_side_effects=True, vmem_limit_bytes=60 * 2**20
        ),
        name="sternheimer",
    )(
        columns.reshape(COLS, ROWS, NX),
        potential.reshape(ROWS, NX),
        orbitals.reshape(ORBS, ROWS, NX),
    )
    return projected.reshape(columns.shape), correlation


def solution(mesh):
    placed = (
        P("band", "space", None, None),
        P("space", None, None),
        P("band", "space", None, None),
    )
    return jax.shard_map(
        shards,
        mesh=mesh,
        in_specs=placed,
        out_specs=(P("band", "space", None, None), P("band", None)),
        check_vma=False,
    )
```

```python
import jax
import jax.numpy as jnp
from jax import lax
from jax.experimental import pallas as pl
from jax.experimental.pallas import tpu as pltpu
from jax.sharding import PartitionSpec as P

COEFFS = (
    -5369.0 / 1800.0,
    12.0 / 7.0,
    -15.0 / 56.0,
    10.0 / 189.0,
    -1.0 / 112.0,
    2.0 / 1925.0,
    -1.0 / 16632.0,
)

MESH = pl.DeviceIdType.MESH
NZ_RING, NX_RING = 8, 4
COLS, ORBS = 4, 32
PLANES, NY, NX = 6, 32, 128
ROWS = PLANES * NY
PART = 16
SPLIT = 8 * PART

STEPS = ((0, 0), (0, 1), (1, 0), (1, 1), (3, 0), (3, 1), (2, 0), (2, 1))
STEPS_Y = ((0, 0), (0, 1), (1, 0), (1, 1))


def kernel(
    col_hbm, pot_hbm, orb_hbm, proj_ref, corr_ref,
    colv, potv, halo, app, phibuf, phi, acol, ahl, cpart, cin, zin, ctot, cts, cts_y,
    rsend, rrecv, rown, fin, ry, ryin, rysum, fin_y, rem,
    loc_sem, near_sem, orb_s, orb_r, h_s, h_r, col_s, col_r, fwd_s, fwd_r,
    orby_s, orby_r, coly_s, coly_r, gat_s, gat_r,
    s1_s, s1_r, s2_s, s2_r, s3_s, s3_r, ry_s, ry_r, fin_s, fin_r, rx_s, rx_r, finy_s, finy_r,
):
    s, b = lax.axis_index("space"), lax.axis_index("band")
    z, h = s // 2, s % 2
    x, yl, c = b // 4, (b // 2) % 2, b % 2
    me = x * 2 + c

    def dev(dz=0, dh=0, dx=0, dy=0, dc=0):
        return (
            ((z + dz) % NZ_RING) * 2 + (h + dh) % 2,
            ((x + dx) % NX_RING) * 4 + ((yl + dy) % 2) * 2 + (c + dc) % 2,
        )

    def part_of(dx, dc):
        return ((x + dx) % NX_RING) * 2 + (c + dc) % 2

    def rows_of(g):
        return pl.ds(pl.multiple_of(g * PART, PART), PART)

    def rows_y(dy, dc):
        g = ((yl + dy) % 2) * 2 + (c + dc) % 2
        return pl.ds(pl.multiple_of(SPLIT + g * PART, PART), PART)

    def slot_of(side, g):
        return pl.ds((side * 8 + g) * COLS, COLS)

    def signal(sem, to):
        pl.semaphore_signal(sem, inc=1, device_id=to, device_id_type=MESH)

    partner = dev(dy=1)
    same_z = dev(dh=1)

    barrier = pltpu.get_barrier_semaphore()
    peers = [dev(dx=dx, dc=dc) for dx, dc in STEPS[1:]]
    peers += [partner, dev(dy=1, dc=1), same_z, dev(dz=1), dev(dz=NZ_RING - 1)]
    for peer in peers:
        signal(barrier, peer)

    load_col = pltpu.make_async_copy(col_hbm, colv, loc_sem.at[0])
    load_col.start()
    load_pot = pltpu.make_async_copy(pot_hbm, potv, loc_sem.at[4])
    load_pot.start()
    load_orb = pltpu.make_async_copy(orb_hbm.at[:, rows_of(me), :], phibuf.at[pl.ds(0, ORBS)], loc_sem.at[1])
    load_orb.start()
    load_orb_y = pltpu.make_async_copy(orb_hbm.at[:, rows_y(0, 0), :], phibuf.at[pl.ds(8 * ORBS, ORBS)], loc_sem.at[5])
    load_orb_y.start()

    pl.semaphore_wait(barrier, len(peers))

    signal(near_sem.at[0], dev(dz=1))
    signal(near_sem.at[1], dev(dz=NZ_RING - 1))

    def halo_copy(n, from_here, to, sem):
        j, rows = n // 2, pl.ds(n % 2 * (ROWS // 2), ROWS // 2)
        source = col_hbm.at[j, rows] if from_here else halo.at[1 - h, j, rows]
        return pltpu.make_async_remote_copy(
            source, halo.at[h, j, rows], h_s.at[sem], h_r.at[sem], device_id=to, device_id_type=MESH
        )

    beside = ((z + 1 - 2 * h + NZ_RING) % NZ_RING) * 2 + h, b
    to_same = [halo_copy(n, True, same_z, n) for n in range(2 * COLS)]
    onward = [halo_copy(n, False, beside, 2 * COLS + n) for n in range(2 * COLS)]

    def pass_on(first, last):
        for n in range(first, last):
            to_same[n].wait_recv()
            onward[n].start()
            if n + 4 < 2 * COLS:
                to_same[n + 4].start()

    for copy in to_same[:4]:
        copy.start()

    orbs = {}
    for i, (dx, dc) in enumerate(STEPS):
        if i > 0:
            orbs[i] = pltpu.make_async_remote_copy(
                orb_hbm.at[:, rows_of(part_of(dx, dc)), :],
                phibuf.at[pl.ds(i * ORBS, ORBS)],
                orb_s.at[i],
                orb_r.at[i],
                device_id=dev(dx=dx, dc=dc),
                device_id_type=MESH,
            )
    orbs_y = {}
    for i, (dy, dc) in enumerate(STEPS_Y):
        if i > 0:
            orbs_y[i] = pltpu.make_async_remote_copy(
                orb_hbm.at[:, rows_y(dy, dc), :],
                phibuf.at[pl.ds((8 + i) * ORBS, ORBS)],
                orby_s.at[i],
                orby_r.at[i],
                device_id=dev(dy=dy, dc=dc),
                device_id_type=MESH,
            )
    for i in (2, 4, 3, 5, 1):
        orbs[i].start()
    orbs_y[1].start()
    orbs[6].start()

    load_col.wait()
    load_pot.wait()

    def local_terms(j, carry):
        planes = [colv[j, pl.ds(p * NY, NY), :] for p in range(PLANES)]
        for p in range(PLANES):
            v = planes[p]
            total = (potv[pl.ds(p * NY, NY), :] - 1.5 * COEFFS[0]) * v
            for k in range(1, 7):
                along = pltpu.roll(v, k, 0) + pltpu.roll(v, NY - k, 0)
                along = along + (pltpu.roll(v, k, 1) + pltpu.roll(v, NX - k, 1))
                if p - k >= 0:
                    along = along + planes[p - k]
                if p + k < PLANES:
                    along = along + planes[p + k]
                total = total + (-0.5 * COEFFS[k]) * along
            app[j, pl.ds(p * NY, NY), :] = total
        return carry

    lax.fori_loop(0, 2, local_terms, 0)
    pass_on(0, 2)
    lax.fori_loop(2, COLS, local_terms, 0)
    pass_on(2, 8)

    def split(value):
        high = value.astype(jnp.bfloat16)
        return high, (value - high.astype(jnp.float32)).astype(jnp.bfloat16)

    def lay_out(ref, store, r0, blocks):
        def one(r, carry):
            rows = pl.ds(pl.multiple_of(r0 + r * 16, 16), 16)
            for q0 in range(0, PART, 8):
                high, low = split(jnp.swapaxes(ref[rows, q0 : q0 + 8, :], 0, 1))
                for q in range(8):
                    store(r0 + r * 16, pl.ds((q0 + q) * NX, NX), high[q], low[q])
            return carry

        lax.fori_loop(0, blocks, one, 0)

    def store_orbitals(row, at, high, low):
        rows = pl.ds(pl.multiple_of(row, 16), 16)
        phi[0, rows, at] = high
        phi[1, rows, at] = low

    def columns_to(mode):
        def store(row, at, high, low):
            ahl[mode, pl.ds(pl.multiple_of(row, 16), 16), at] = high
            ahl[mode, pl.ds(pl.multiple_of(64 + row, 16), 16), at] = low

        return store

    orbs_y[2].start()
    load_orb.wait()
    orbs[1].wait_recv()
    lay_out(phibuf, store_orbitals, 0, 4)
    load_orb_y.wait()
    orbs_y[1].wait_recv()
    lay_out(phibuf, store_orbitals, 256, 4)
    for i in (0, 1):
        pl.semaphore_wait(near_sem.at[i], 1)
    signal(near_sem.at[2], dev(dz=2))
    signal(near_sem.at[3], dev(dz=NZ_RING - 2))

    for copy in onward:
        copy.wait_recv()

    def halo_terms(j, carry):
        for p in range(PLANES):
            total = app[j, pl.ds(p * NY, NY), :]
            for k in range(1, 7):
                if p - k < 0:
                    total = total + (-0.5 * COEFFS[k]) * halo[0, j, pl.ds((p - k + PLANES) * NY, NY), :]
                if p + k >= PLANES:
                    total = total + (-0.5 * COEFFS[k]) * halo[1, j, pl.ds((p + k - PLANES) * NY, NY), :]
            app[j, pl.ds(p * NY, NY), :] = total
        return carry

    lax.fori_loop(0, COLS, halo_terms, 0)

    own_col = pltpu.make_async_copy(app.at[:, rows_of(me), :], acol.at[0, slot_of(yl, me)], loc_sem.at[2])
    own_col.start()
    own_col_y = pltpu.make_async_copy(app.at[:, rows_y(0, 0), :], acol.at[1, slot_of(yl, me)], loc_sem.at[6])
    own_col_y.start()
    cols, fwds, cols_y, gathers = {}, {}, {}, {}
    for i, (dx, dc) in enumerate(STEPS):
        if i > 0:
            cols[i] = pltpu.make_async_remote_copy(
                app.at[:, rows_of(part_of(dx, dc)), :],
                acol.at[0, slot_of(yl, me)],
                col_s.at[i],
                col_r.at[i],
                device_id=dev(dx=dx, dc=dc),
                device_id_type=MESH,
            )
        came = slot_of(yl, part_of(-dx, -dc))
        fwds[i] = pltpu.make_async_remote_copy(
            app.at[:, rows_of(me), :] if i == 0 else acol.at[0, came],
            acol.at[0, came],
            fwd_s.at[i],
            fwd_r.at[i],
            device_id=partner,
            device_id_type=MESH,
        )
    for i, (dy, dc) in enumerate(STEPS_Y):
        if i > 0:
            cols_y[i] = pltpu.make_async_remote_copy(
                app.at[:, rows_y(dy, dc), :],
                acol.at[1, slot_of(yl, me)],
                coly_s.at[i],
                coly_r.at[i],
                device_id=dev(dy=dy, dc=dc),
                device_id_type=MESH,
            )
    def block(dx, dy):
        return acol.at[1, pl.ds(((yl + dy) % 2) * 32 + ((x + dx) % NX_RING) * 8, 8)]

    def gather(n, at, dy, to):
        return pltpu.make_async_remote_copy(
            block(at, dy), block(at, dy), gat_s.at[n], gat_r.at[n], device_id=dev(dx=to), device_id_type=MESH
        )

    for dy in (0, 1):
        gathers[1, dy] = gather(dy, 0, dy, 1)
        gathers[3, dy] = gather(2 + dy, 0, dy, 3)
    gathers[2, 0] = gather(4, 3, 0, 1)
    gathers[2, 1] = gather(5, 1, 1, 3)
    for i in (6, 7, 2, 4, 3, 5, 1):
        cols[i].start()
    for i in (2, 3, 1):
        cols_y[i].start()
    orbs_y[3].start()
    fwds[0].start()
    orbs[7].start()
    for i in (2, 4, 3, 5):
        orbs[i].wait_recv()
    lay_out(phibuf, store_orbitals, 64, 8)
    own_col_y.wait()
    cols_y[1].wait_recv()
    for dx in (1, 3):
        gathers[dx, 0].start()
    for i in (1, 2, 4, 3, 5):
        cols[i].wait_recv()
        fwds[i].start()
    for i in (2, 3):
        cols_y[i].wait_recv()
    for dx in (1, 3):
        gathers[dx, 1].start()
    gathers[1, 0].wait_recv()
    gathers[2, 0].start()
    for i in (6, 7):
        cols[i].wait_recv()
        fwds[i].start()
    gathers[3, 1].wait_recv()
    gathers[2, 1].start()

    own_col.wait()
    lay_out(acol.at[0], columns_to(0), yl * 32, 2)
    orbs[6].wait_recv()
    lay_out(phibuf, store_orbitals, 192, 2)
    orbs_y[2].wait_recv()
    lay_out(phibuf, store_orbitals, 320, 2)
    orbs[7].wait_recv()
    lay_out(phibuf, store_orbitals, 224, 2)
    orbs_y[3].wait_recv()
    lay_out(phibuf, store_orbitals, 352, 2)
    for i in range(8):
        fwds[i].wait_recv()
    lay_out(acol.at[0], columns_to(0), 32 - yl * 32, 2)

    half_lanes = lax.broadcasted_iota(jnp.int32, (16, 128), 1) < 64
    dims = (((1,), (1,)), ((), ()))

    def correlate(mode, i0, n):
        rows = pl.ds(i0 * ORBS, n * ORBS)
        high = lax.dot_general(phi[0, rows, :], ahl[mode], dims, preferred_element_type=jnp.float32)
        low = lax.dot_general(phi[1, rows, :], ahl[mode], dims, preferred_element_type=jnp.float32)
        value = high + pltpu.roll(high, 64, 1) + low
        for i in range(n):
            first = value[i * ORBS : i * ORBS + 16]
            second = value[i * ORBS + 16 : i * ORBS + 32]
            packed = jnp.where(half_lanes, first, pltpu.roll(second, 64, 1))
            if i0 + i in (8, 9):
                cpart[i0 + i - 8, 0] += packed[:8]
                cpart[i0 + i - 8, 1] += packed[8:]
            else:
                cpart[i0 + i, 0] = packed[:8]
                cpart[i0 + i, 1] = packed[8:]

    sums = {}

    def send_parts(i):
        if i < 8:
            dx, dc = STEPS[i]
            dy, n0 = 0, i * 2
        else:
            dx, (dy, dc) = 0, STEPS_Y[i - 8]
            n0 = i * 2 - 4
        for dh in (0, 1):
            if (i, dh) != (0, 0):
                n = n0 + dh
                sums[n] = pltpu.make_async_remote_copy(
                    cpart.at[i, (h + dh) % 2],
                    cin.at[n],
                    s1_s.at[n],
                    s1_r.at[n],
                    device_id=dev(dx=-dx, dy=dy, dc=-dc, dh=dh),
                    device_id_type=MESH,
                )
                sums[n].start()

    correlate(0, 0, 8)
    for i in (6, 7, 2, 4, 3, 5):
        send_parts(i)
    for n in ((3, 0), (1, 1), (2, 0), (2, 1)):
        gathers[n].wait_recv()
    lay_out(acol.at[1], columns_to(1), 0, 4)
    correlate(1, 8, 4)
    for i in (10, 11, 1, 0):
        send_parts(i)

    total = cpart[0, h]
    for n in range(1, 20):
        sums[n].wait_recv()
        total = total + cin[n]

    zin[z] = total
    for i in (2, 3):
        pl.semaphore_wait(near_sem.at[i], 1)
    zs = []
    for dz in (4, 3, 5, 2, 6, 1, 7):
        copy = pltpu.make_async_remote_copy(
            zin.at[z], zin.at[z], s2_s.at[dz], s2_r.at[dz], device_id=dev(dz=dz), device_id_type=MESH
        )
        copy.start()
        zs.append(copy)
    for copy in zs:
        copy.wait_recv()
    total = zin[0]
    for n in range(1, NZ_RING):
        total = total + zin[n]

    ctot[0, h] = total
    backs = []
    users = [(i, dx, 0, dc) for i, (dx, dc) in enumerate(STEPS)]
    users += [(8, 0, 1, 0), (9, 0, 1, 1)]
    for i in (6, 7, 8, 9, 2, 4, 3, 5, 1, 0):
        _, dx, dy, dc = users[i]
        for dh in (1, 0):
            if (i, dh) != (0, 0):
                n = i * 2 + dh
                copy = pltpu.make_async_remote_copy(
                    ctot.at[0, h],
                    ctot.at[i, h],
                    s3_s.at[n],
                    s3_r.at[n],
                    device_id=dev(dx=dx, dy=dy, dc=dc, dh=dh),
                    device_id_type=MESH,
                )
                copy.start()
                backs.append(copy)
    for copy in backs:
        copy.wait_recv()

    packed = ctot[...].reshape(10, 16, 128)
    swapped = pltpu.roll(packed.reshape(160, 128), 64, 1).reshape(10, 16, 128)
    corr = jnp.concatenate([packed, swapped], axis=1).reshape(320, 128)
    corr_y = jnp.concatenate([corr[:64], corr[256:]], axis=0)

    def operands(value, out):
        high, low = split(jnp.transpose(value)[:64])
        for side in (0, 1):
            out[side, pl.ds(0, 32), :] = high[side * 32 : side * 32 + 32]
            out[side, pl.ds(32, 32), :] = low[side * 32 : side * 32 + 32]

    def removed(left, rows, side, out):
        for q0 in range(0, PART, 4):
            at = pl.ds(q0 * NX, 4 * NX)
            both = jnp.dot(left[side], phi[0, rows, at], preferred_element_type=jnp.float32)
            rest = jnp.dot(left[side, pl.ds(0, 32), :], phi[1, rows, at], preferred_element_type=jnp.float32)
            value = both[:32] + both[32:] + rest
            for q in range(4):
                for k in range(NX_RING):
                    out(k, q0 + q, value[k * 8 : k * 8 + 8, q * NX : (q + 1) * NX])

    def to_send(k, q, value):
        rsend[k, q] = value

    def to_own(k, q, value):
        rown[k, q] = value

    first, last = pl.ds(0, 256), pl.ds(256, 128)
    operands(corr_y, cts_y)
    for side in (0, 1):

        def to_x(k, q, value):
            ry[k, side, q] = value

        removed(cts_y, last, side, to_x)

    def along_x(n, source, dx):
        return pltpu.make_async_remote_copy(
            source, ryin.at[n], rx_s.at[n], rx_r.at[n], device_id=dev(dx=dx), device_id_type=MESH
        )

    up, down = (x + 1) % NX_RING, (x + 3) % NX_RING
    xs = {
        0: along_x(0, ry.at[(x + 2) % NX_RING, 0], 1),
        1: along_x(1, ry.at[(x + 2) % NX_RING, 1], 3),
        2: along_x(2, ry.at[up, 1], 1),
        3: along_x(3, ry.at[down, 0], 3),
        4: along_x(4, rysum.at[0], 1),
        5: along_x(5, rysum.at[1], 3),
    }
    for n in range(4):
        xs[n].start()
    operands(corr[:256], cts)
    removed(cts, first, 1 - yl, to_send)
    order = (2, 1, 3, 0)
    ys = {}
    for dx in order:
        k = (x + dx) % NX_RING
        ys[dx] = pltpu.make_async_remote_copy(
            rsend.at[k], rrecv.at[k], ry_s.at[dx], ry_r.at[dx], device_id=partner, device_id_type=MESH
        )
        ys[dx].start()
    for n, to in ((0, up), (1, down)):
        xs[n].wait_recv()
        rysum[n] = ry[to, n] + ryin[n]
        xs[4 + n].start()
    removed(cts, first, yl, to_own)

    own = corr[:32]
    lane = lax.broadcasted_iota(jnp.int32, (ORBS, 128), 1)
    value = own
    for side in (0, 1):
        for k in range(NX_RING):
            source, target = side * 32 + k * 8, k * 16 + side * 8
            if source != target:
                moved = pltpu.roll(own, (target - source) % 128, 1)
                value = jnp.where((lane >= target) & (lane < target + 8), moved, value)
    corr_ref[...] = value[:, :64]

    fins = {}
    for dx in order:
        k = (x + dx) % NX_RING
        ys[dx].wait_recv()
        fin[k] = jnp.swapaxes(rown[k] + rrecv[k], 0, 1)
        for dc in (1, 0):
            source = fin.at[k, pl.ds(((c + dc) % 2) * COLS, COLS)]
            target = rem.at[:, rows_of(me), :]
            n = STEPS.index((dx, dc))
            if n == 0:
                local = pltpu.make_async_copy(source, target, loc_sem.at[3])
                local.start()
            else:
                fins[n] = pltpu.make_async_remote_copy(
                    source, target, fin_s.at[n], fin_r.at[n], device_id=dev(dx=dx, dc=dc), device_id_type=MESH
                )
                fins[n].start()
    for side, n, m in ((0, 3, 4), (1, 2, 5)):
        xs[n].wait_recv()
        xs[m].wait_recv()
        fin_y[side] = jnp.swapaxes(ry[x, side] + ryin[n] + ryin[m], 0, 1)
    for i in (2, 3, 1, 0):
        dy, dc = STEPS_Y[i]
        source = fin_y.at[(yl + dy) % 2, pl.ds(((c + dc) % 2) * COLS, COLS)]
        target = rem.at[:, rows_y(0, 0), :]
        if i == 0:
            local_y = pltpu.make_async_copy(source, target, loc_sem.at[7])
            local_y.start()
        else:
            fins[8 + i] = pltpu.make_async_remote_copy(
                source, target, finy_s.at[i], finy_r.at[i], device_id=dev(dy=dy, dc=dc), device_id_type=MESH
            )
            fins[8 + i].start()
    local.wait()
    local_y.wait()
    for copy in fins.values():
        copy.wait_recv()
    proj_ref[...] = app[...] - rem[...]

    groups = [to_same, onward, zs, backs]
    groups += [g.values() for g in (orbs, orbs_y, cols, fwds, cols_y, gathers, sums, ys, xs, fins)]
    for group in groups:
        for copy in group:
            copy.wait_send()


def shards(columns, potential, orbitals):
    f32, bf16 = jnp.float32, jnp.bfloat16
    dma = pltpu.SemaphoreType.DMA
    scratch = [
        pltpu.VMEM((COLS, ROWS, NX), f32),
        pltpu.VMEM((ROWS, NX), f32),
        pltpu.VMEM((2, COLS, ROWS, NX), f32),
        pltpu.VMEM((COLS, ROWS, NX), f32),
        pltpu.VMEM((12 * ORBS, PART, NX), f32),
        pltpu.VMEM((2, 12 * ORBS, PART * NX), bf16),
        pltpu.VMEM((2, 64, PART, NX), f32),
        pltpu.VMEM((2, 128, PART * NX), bf16),
        pltpu.VMEM((12, 2, 8, 128), f32),
        pltpu.VMEM((20, 8, 128), f32),
        pltpu.VMEM((NZ_RING, 8, 128), f32),
        pltpu.VMEM((10, 2, 8, 128), f32),
        pltpu.VMEM((2, 64, 256), bf16),
        pltpu.VMEM((2, 64, 128), bf16),
        pltpu.VMEM((NX_RING, PART, 8, NX), f32),
        pltpu.VMEM((NX_RING, PART, 8, NX), f32),
        pltpu.VMEM((NX_RING, PART, 8, NX), f32),
        pltpu.VMEM((NX_RING, 8, PART, NX), f32),
        pltpu.VMEM((NX_RING, 2, PART, 8, NX), f32),
        pltpu.VMEM((6, PART, 8, NX), f32),
        pltpu.VMEM((2, PART, 8, NX), f32),
        pltpu.VMEM((2, 8, PART, NX), f32),
        pltpu.VMEM((COLS, ROWS, NX), f32),
        dma((8,)),
        pltpu.SemaphoreType.REGULAR((4,)),
        dma((8,)), dma((8,)),
        dma((16,)), dma((16,)),
        dma((8,)), dma((8,)),
        dma((8,)), dma((8,)),
        dma((4,)), dma((4,)),
        dma((4,)), dma((4,)),
        dma((8,)), dma((8,)),
        dma((20,)), dma((20,)),
        dma((8,)), dma((8,)),
        dma((20,)), dma((20,)),
        dma((4,)), dma((4,)),
        dma((8,)), dma((8,)),
        dma((6,)), dma((6,)),
        dma((4,)), dma((4,)),
    ]
    vmem, anywhere = pl.BlockSpec(memory_space=pltpu.VMEM), pl.BlockSpec(memory_space=pl.ANY)
    projected, correlation = pl.pallas_call(
        kernel,
        out_shape=(
            jax.ShapeDtypeStruct((COLS, ROWS, NX), f32),
            jax.ShapeDtypeStruct((ORBS, 64), f32),
        ),
        in_specs=[anywhere, anywhere, anywhere],
        out_specs=(vmem, vmem),
        scratch_shapes=scratch,
        compiler_params=pltpu.CompilerParams(
            collective_id=0, has_side_effects=True, vmem_limit_bytes=40 * 2**20
        ),
        name="sternheimer",
    )(
        pltpu.with_memory_space_constraint(columns.reshape(COLS, ROWS, NX), pltpu.HBM),
        pltpu.with_memory_space_constraint(potential.reshape(ROWS, NX), pltpu.HBM),
        pltpu.with_memory_space_constraint(orbitals.reshape(ORBS, ROWS, NX), pltpu.HBM),
    )
    return projected.reshape(columns.shape), correlation


def solution(mesh):
    placed = (
        P("band", "space", None, None),
        P("space", None, None),
        P("band", "space", None, None),
    )
    return jax.shard_map(
        shards,
        mesh=mesh,
        in_specs=placed,
        out_specs=(P("band", "space", None, None), P("band", None)),
        check_vma=False,
    )
```

```python
import jax
import jax.numpy as jnp
from jax import lax
from jax.experimental import pallas as pl
from jax.experimental.pallas import tpu as pltpu
from jax.sharding import PartitionSpec as P

COEFFS = (
    -5369.0 / 1800.0,
    12.0 / 7.0,
    -15.0 / 56.0,
    10.0 / 189.0,
    -1.0 / 112.0,
    2.0 / 1925.0,
    -1.0 / 16632.0,
)

MESH = pl.DeviceIdType.MESH
NZ_RING, NX_RING = 8, 4
COLS, ORBS = 4, 32
PLANES, NY, NX = 6, 32, 128
ROWS = PLANES * NY
PART = 16
SPLIT = 8 * PART

STEPS = ((0, 0), (0, 1), (1, 0), (1, 1), (3, 0), (3, 1), (2, 0), (2, 1))
STEPS_Y = ((0, 0), (0, 1), (1, 0), (1, 1))


def kernel(
    col_hbm, pot_hbm, orb_hbm, proj_ref, corr_ref,
    colv, potv, halo, app, phibuf, phi, acol, ahl, cpart, cin, zin, ctot, cts, cts_y,
    rx, rrecv, fin, ry, ryin, rysum, fin_y, rem,
    loc_sem, near_sem, orb_s, orb_r, h_s, h_r, col_s, col_r, fwd_s, fwd_r,
    orby_s, orby_r, coly_s, coly_r, gat_s, gat_r,
    s1_s, s1_r, s2_s, s2_r, s3_s, s3_r, ry_s, ry_r, fin_s, fin_r, rx_s, rx_r, finy_s, finy_r,
):
    s, b = lax.axis_index("space"), lax.axis_index("band")
    z, h = s // 2, s % 2
    x, yl, c = b // 4, (b // 2) % 2, b % 2
    me = x * 2 + c

    def dev(dz=0, dh=0, dx=0, dy=0, dc=0):
        return (
            ((z + dz) % NZ_RING) * 2 + (h + dh) % 2,
            ((x + dx) % NX_RING) * 4 + ((yl + dy) % 2) * 2 + (c + dc) % 2,
        )

    def part_of(dx, dc):
        return ((x + dx) % NX_RING) * 2 + (c + dc) % 2

    def rows_of(g):
        return pl.ds(pl.multiple_of(g * PART, PART), PART)

    def rows_y(dy, dc):
        g = ((yl + dy) % 2) * 2 + (c + dc) % 2
        return pl.ds(pl.multiple_of(SPLIT + g * PART, PART), PART)

    def slot_of(side, g):
        return pl.ds((side * 8 + g) * COLS, COLS)

    def signal(sem, to):
        pl.semaphore_signal(sem, inc=1, device_id=to, device_id_type=MESH)

    partner = dev(dy=1)
    same_z = dev(dh=1)

    barrier = pltpu.get_barrier_semaphore()
    peers = [dev(dx=dx, dc=dc) for dx, dc in STEPS[1:]]
    peers += [partner, dev(dy=1, dc=1), same_z, dev(dz=1), dev(dz=NZ_RING - 1)]
    for peer in peers:
        signal(barrier, peer)

    load_col = pltpu.make_async_copy(col_hbm, colv, loc_sem.at[0])
    load_col.start()
    load_pot = pltpu.make_async_copy(pot_hbm, potv, loc_sem.at[4])
    load_pot.start()
    load_orb = pltpu.make_async_copy(orb_hbm.at[:, rows_of(me), :], phibuf.at[pl.ds(0, ORBS)], loc_sem.at[1])
    load_orb.start()
    load_orb_y = pltpu.make_async_copy(orb_hbm.at[:, rows_y(0, 0), :], phibuf.at[pl.ds(8 * ORBS, ORBS)], loc_sem.at[5])
    load_orb_y.start()

    pl.semaphore_wait(barrier, len(peers))

    signal(near_sem.at[0], dev(dz=1))
    signal(near_sem.at[1], dev(dz=NZ_RING - 1))

    def halo_copy(n, from_here, to, sem):
        j, rows = n // 2, pl.ds(n % 2 * (ROWS // 2), ROWS // 2)
        source = col_hbm.at[j, rows] if from_here else halo.at[1 - h, j, rows]
        return pltpu.make_async_remote_copy(
            source, halo.at[h, j, rows], h_s.at[sem], h_r.at[sem], device_id=to, device_id_type=MESH
        )

    beside = ((z + 1 - 2 * h + NZ_RING) % NZ_RING) * 2 + h, b
    to_same = [halo_copy(n, True, same_z, n) for n in range(2 * COLS)]
    onward = [halo_copy(n, False, beside, 2 * COLS + n) for n in range(2 * COLS)]

    def pass_on(first, last):
        for n in range(first, last):
            to_same[n].wait_recv()
            onward[n].start()
            if n + 4 < 2 * COLS:
                to_same[n + 4].start()

    for copy in to_same[:4]:
        copy.start()

    orbs = {}
    for i, (dx, dc) in enumerate(STEPS):
        if i > 0:
            orbs[i] = pltpu.make_async_remote_copy(
                orb_hbm.at[:, rows_of(part_of(dx, dc)), :],
                phibuf.at[pl.ds(i * ORBS, ORBS)],
                orb_s.at[i],
                orb_r.at[i],
                device_id=dev(dx=dx, dc=dc),
                device_id_type=MESH,
            )
    orbs_y = {}
    for i, (dy, dc) in enumerate(STEPS_Y):
        if i > 0:
            orbs_y[i] = pltpu.make_async_remote_copy(
                orb_hbm.at[:, rows_y(dy, dc), :],
                phibuf.at[pl.ds((8 + i) * ORBS, ORBS)],
                orby_s.at[i],
                orby_r.at[i],
                device_id=dev(dy=dy, dc=dc),
                device_id_type=MESH,
            )
    for i in (2, 4, 3, 5, 1):
        orbs[i].start()
    orbs_y[1].start()
    orbs[6].start()

    load_col.wait()
    load_pot.wait()

    def local_terms(j, carry):
        planes = [colv[j, pl.ds(p * NY, NY), :] for p in range(PLANES)]
        for p in range(PLANES):
            v = planes[p]
            total = (potv[pl.ds(p * NY, NY), :] - 1.5 * COEFFS[0]) * v
            for k in range(1, 7):
                along = pltpu.roll(v, k, 0) + pltpu.roll(v, NY - k, 0)
                along = along + (pltpu.roll(v, k, 1) + pltpu.roll(v, NX - k, 1))
                if p - k >= 0:
                    along = along + planes[p - k]
                if p + k < PLANES:
                    along = along + planes[p + k]
                total = total + (-0.5 * COEFFS[k]) * along
            app[j, pl.ds(p * NY, NY), :] = total
        return carry

    lax.fori_loop(0, 2, local_terms, 0)
    pass_on(0, 2)
    lax.fori_loop(2, COLS, local_terms, 0)
    pass_on(2, 8)

    def split(value):
        high = value.astype(jnp.bfloat16)
        return high, (value - high.astype(jnp.float32)).astype(jnp.bfloat16)

    def lay_out(ref, store, r0, blocks):
        def one(r, carry):
            rows = pl.ds(pl.multiple_of(r0 + r * 16, 16), 16)
            for q0 in range(0, PART, 8):
                high, low = split(jnp.swapaxes(ref[rows, q0 : q0 + 8, :], 0, 1))
                for q in range(8):
                    store(r0 + r * 16, pl.ds((q0 + q) * NX, NX), high[q], low[q])
            return carry

        lax.fori_loop(0, blocks, one, 0)

    def orbitals_to(base, n):
        def store(row, at, high, low):
            k = (row - base) // 16
            rows = pl.ds(pl.multiple_of(base + k % 2 * (n * 16) + k // 2 * 16, 16), 16)
            phi[0, rows, at] = high
            phi[1, rows, at] = low

        return store

    first_rows, last_rows = orbitals_to(0, 8), orbitals_to(256, 4)

    def columns_to(mode):
        def store(row, at, high, low):
            ahl[mode, pl.ds(pl.multiple_of(row, 16), 16), at] = high
            ahl[mode, pl.ds(pl.multiple_of(64 + row, 16), 16), at] = low

        return store

    orbs_y[2].start()
    load_orb.wait()
    orbs[1].wait_recv()
    lay_out(phibuf, first_rows, 0, 4)
    load_orb_y.wait()
    orbs_y[1].wait_recv()
    lay_out(phibuf, last_rows, 256, 4)
    for i in (0, 1):
        pl.semaphore_wait(near_sem.at[i], 1)
    signal(near_sem.at[2], dev(dz=2))
    signal(near_sem.at[3], dev(dz=NZ_RING - 2))

    for copy in onward:
        copy.wait_recv()

    def halo_terms(j, carry):
        for p in range(PLANES):
            total = app[j, pl.ds(p * NY, NY), :]
            for k in range(1, 7):
                if p - k < 0:
                    total = total + (-0.5 * COEFFS[k]) * halo[0, j, pl.ds((p - k + PLANES) * NY, NY), :]
                if p + k >= PLANES:
                    total = total + (-0.5 * COEFFS[k]) * halo[1, j, pl.ds((p + k - PLANES) * NY, NY), :]
            app[j, pl.ds(p * NY, NY), :] = total
        return carry

    lax.fori_loop(0, COLS, halo_terms, 0)

    own_col = pltpu.make_async_copy(app.at[:, rows_of(me), :], acol.at[0, slot_of(yl, me)], loc_sem.at[2])
    own_col.start()
    own_col_y = pltpu.make_async_copy(app.at[:, rows_y(0, 0), :], acol.at[1, slot_of(yl, me)], loc_sem.at[6])
    own_col_y.start()
    cols, fwds, cols_y, gathers = {}, {}, {}, {}
    for i, (dx, dc) in enumerate(STEPS):
        if i > 0:
            cols[i] = pltpu.make_async_remote_copy(
                app.at[:, rows_of(part_of(dx, dc)), :],
                acol.at[0, slot_of(yl, me)],
                col_s.at[i],
                col_r.at[i],
                device_id=dev(dx=dx, dc=dc),
                device_id_type=MESH,
            )
        came = slot_of(yl, part_of(-dx, -dc))
        fwds[i] = pltpu.make_async_remote_copy(
            app.at[:, rows_of(me), :] if i == 0 else acol.at[0, came],
            acol.at[0, came],
            fwd_s.at[i],
            fwd_r.at[i],
            device_id=partner,
            device_id_type=MESH,
        )
    for i, (dy, dc) in enumerate(STEPS_Y):
        if i > 0:
            cols_y[i] = pltpu.make_async_remote_copy(
                app.at[:, rows_y(dy, dc), :],
                acol.at[1, slot_of(yl, me)],
                coly_s.at[i],
                coly_r.at[i],
                device_id=dev(dy=dy, dc=dc),
                device_id_type=MESH,
            )
    def block(dx, dy):
        return acol.at[1, pl.ds(((yl + dy) % 2) * 32 + ((x + dx) % NX_RING) * 8, 8)]

    def gather(n, at, dy, to):
        return pltpu.make_async_remote_copy(
            block(at, dy), block(at, dy), gat_s.at[n], gat_r.at[n], device_id=dev(dx=to), device_id_type=MESH
        )

    for dy in (0, 1):
        gathers[1, dy] = gather(dy, 0, dy, 1)
        gathers[3, dy] = gather(2 + dy, 0, dy, 3)
    gathers[2, 0] = gather(4, 3, 0, 1)
    gathers[2, 1] = gather(5, 1, 1, 3)
    for i in (1, 2, 4, 3, 5, 6, 7):
        cols[i].start()
    for i in (2, 3, 1):
        cols_y[i].start()
    orbs_y[3].start()
    fwds[0].start()
    for i in (2, 4, 3, 5):
        orbs[i].wait_recv()
    lay_out(phibuf, first_rows, 64, 8)
    own_col_y.wait()
    cols_y[1].wait_recv()
    for dx in (1, 3):
        gathers[dx, 0].start()
    for i in (1, 2, 4, 3, 5):
        cols[i].wait_recv()
        fwds[i].start()
    for i in (2, 3):
        cols_y[i].wait_recv()
    for dx in (1, 3):
        gathers[dx, 1].start()
    orbs[7].start()
    gathers[1, 0].wait_recv()
    gathers[2, 0].start()
    for i in (6, 7):
        cols[i].wait_recv()
        fwds[i].start()
    gathers[3, 1].wait_recv()
    gathers[2, 1].start()

    own_col.wait()
    lay_out(acol.at[0], columns_to(0), yl * 32, 2)
    orbs[6].wait_recv()
    lay_out(phibuf, first_rows, 192, 2)
    orbs_y[2].wait_recv()
    lay_out(phibuf, last_rows, 320, 2)
    orbs[7].wait_recv()
    lay_out(phibuf, first_rows, 224, 2)
    orbs_y[3].wait_recv()
    lay_out(phibuf, last_rows, 352, 2)
    for i in range(8):
        fwds[i].wait_recv()
    lay_out(acol.at[0], columns_to(0), 32 - yl * 32, 2)

    half_lanes = lax.broadcasted_iota(jnp.int32, (16, 128), 1) < 64
    dims = (((1,), (1,)), ((), ()))

    def correlate(mode, i0, n):
        rows = pl.ds(i0 * ORBS, n * ORBS)
        high = lax.dot_general(phi[0, rows, :], ahl[mode], dims, preferred_element_type=jnp.float32)
        low = lax.dot_general(phi[1, rows, :], ahl[mode], dims, preferred_element_type=jnp.float32)
        value = high + pltpu.roll(high, 64, 1) + low
        for i in range(n):
            first = value[i * 16 : i * 16 + 16]
            second = value[(n + i) * 16 : (n + i) * 16 + 16]
            packed = jnp.where(half_lanes, first, pltpu.roll(second, 64, 1))
            if i0 + i in (8, 9):
                cpart[i0 + i - 8, 0] += packed[:8]
                cpart[i0 + i - 8, 1] += packed[8:]
            else:
                cpart[i0 + i, 0] = packed[:8]
                cpart[i0 + i, 1] = packed[8:]

    sums = {}

    def send_parts(i):
        if i < 8:
            dx, dc = STEPS[i]
            dy, n0 = 0, i * 2
        else:
            dx, (dy, dc) = 0, STEPS_Y[i - 8]
            n0 = i * 2 - 4
        for dh in (0, 1):
            if (i, dh) != (0, 0):
                n = n0 + dh
                sums[n] = pltpu.make_async_remote_copy(
                    cpart.at[i, (h + dh) % 2],
                    cin.at[n],
                    s1_s.at[n],
                    s1_r.at[n],
                    device_id=dev(dx=-dx, dy=dy, dc=-dc, dh=dh),
                    device_id_type=MESH,
                )
                sums[n].start()

    correlate(0, 0, 8)
    for i in (6, 7, 2, 4, 3, 5):
        send_parts(i)
    for n in ((3, 0), (1, 1), (2, 0), (2, 1)):
        gathers[n].wait_recv()
    lay_out(acol.at[1], columns_to(1), 0, 4)
    correlate(1, 8, 4)
    for i in (10, 11, 1, 0):
        send_parts(i)

    total = cpart[0, h]
    for n in range(1, 20):
        sums[n].wait_recv()
        total = total + cin[n]

    zin[z] = total
    for i in (2, 3):
        pl.semaphore_wait(near_sem.at[i], 1)
    zs = []
    for dz in (4, 3, 5, 2, 6, 1, 7):
        copy = pltpu.make_async_remote_copy(
            zin.at[z], zin.at[z], s2_s.at[dz], s2_r.at[dz], device_id=dev(dz=dz), device_id_type=MESH
        )
        copy.start()
        zs.append(copy)
    for copy in zs:
        copy.wait_recv()
    total = zin[0]
    for n in range(1, NZ_RING):
        total = total + zin[n]

    ctot[0, h] = total
    backs = []
    users = [(i, dx, 0, dc) for i, (dx, dc) in enumerate(STEPS)]
    users += [(8, 0, 1, 0), (9, 0, 1, 1)]
    for i in (6, 7, 8, 9, 2, 4, 3, 5, 1, 0):
        _, dx, dy, dc = users[i]
        for dh in (1, 0):
            if (i, dh) != (0, 0):
                n = i * 2 + dh
                copy = pltpu.make_async_remote_copy(
                    ctot.at[0, h],
                    ctot.at[i, h],
                    s3_s.at[n],
                    s3_r.at[n],
                    device_id=dev(dx=dx, dy=dy, dc=dc, dh=dh),
                    device_id_type=MESH,
                )
                copy.start()
                backs.append(copy)
    for copy in backs:
        copy.wait_recv()

    def operand(packed, out):
        high, low = split(packed)
        out[pl.ds(0, 64), :] = high
        out[pl.ds(64, 64), :] = low

    def removed(left, rows, out):
        for q0 in range(0, PART, 4):
            at = pl.ds(q0 * NX, 4 * NX)
            both = jnp.dot(left[...], phi[0, rows, at], preferred_element_type=jnp.float32)
            rest = jnp.dot(left[pl.ds(0, 64), :], phi[1, rows, at], preferred_element_type=jnp.float32)
            value = both[:64] + both[64:] + rest
            for q in range(4):
                for side in (0, 1):
                    for k in range(NX_RING):
                        n = side * 32 + k * 8
                        out[side, k, q0 + q] = value[n : n + 8, q * NX : (q + 1) * NX]

    packed = jnp.concatenate([ctot[0:2].reshape(32, 128), ctot[8:10].reshape(32, 128)], axis=0)
    turned = jnp.transpose(jnp.concatenate([packed, packed], axis=0))
    low_lanes = lax.broadcasted_iota(jnp.int32, (64, 128), 1) < 64
    operand(jnp.where(low_lanes, turned[:64], turned[64:]), cts_y)
    removed(cts_y, pl.ds(256, 128), ry)

    def along_x(n, source, dx):
        return pltpu.make_async_remote_copy(
            source, ryin.at[n], rx_s.at[n], rx_r.at[n], device_id=dev(dx=dx), device_id_type=MESH
        )

    up, down = (x + 1) % NX_RING, (x + 3) % NX_RING
    xs = {
        0: along_x(0, ry.at[0, (x + 2) % NX_RING], 1),
        1: along_x(1, ry.at[1, (x + 2) % NX_RING], 3),
        2: along_x(2, ry.at[1, up], 1),
        3: along_x(3, ry.at[0, down], 3),
        4: along_x(4, rysum.at[0], 1),
        5: along_x(5, rysum.at[1], 3),
    }
    for n in range(4):
        xs[n].start()

    turned = jnp.transpose(ctot[0:8].reshape(128, 128))
    operand(jnp.concatenate([turned[:64], turned[64:]], axis=1), cts)
    removed(cts, pl.ds(0, 256), rx)
    order = (2, 1, 3, 0)
    ys = {}
    for dx in order:
        k = (x + dx) % NX_RING
        ys[dx] = pltpu.make_async_remote_copy(
            rx.at[1 - yl, k], rrecv.at[k], ry_s.at[dx], ry_r.at[dx], device_id=partner, device_id_type=MESH
        )
        ys[dx].start()
    for n, to in ((0, up), (1, down)):
        xs[n].wait_recv()
        rysum[n] = ry[n, to] + ryin[n]
        xs[4 + n].start()

    packed = ctot[0].reshape(16, 128)
    own = jnp.concatenate([packed, pltpu.roll(packed, 64, 1)], axis=0)
    lane = lax.broadcasted_iota(jnp.int32, (ORBS, 128), 1)
    value = own
    for side in (0, 1):
        for k in range(NX_RING):
            source, target = side * 32 + k * 8, k * 16 + side * 8
            if source != target:
                moved = pltpu.roll(own, (target - source) % 128, 1)
                value = jnp.where((lane >= target) & (lane < target + 8), moved, value)
    corr_ref[...] = value[:, :64]

    fins = {}

    def finish(dx):
        k = (x + dx) % NX_RING
        ys[dx].wait_recv()
        fin[k] = jnp.swapaxes(rx[yl, k] + rrecv[k], 0, 1)
        for dc in (1, 0):
            source = fin.at[k, pl.ds(((c + dc) % 2) * COLS, COLS)]
            target = rem.at[:, rows_of(me), :]
            n = STEPS.index((dx, dc))
            if n == 0:
                fins[n] = pltpu.make_async_copy(source, target, loc_sem.at[3])
            else:
                fins[n] = pltpu.make_async_remote_copy(
                    source, target, fin_s.at[n], fin_r.at[n], device_id=dev(dx=dx, dc=dc), device_id_type=MESH
                )
            fins[n].start()

    for dx in order[:3]:
        finish(dx)
    for side, n, m in ((0, 3, 4), (1, 2, 5)):
        xs[n].wait_recv()
        xs[m].wait_recv()
        fin_y[side] = jnp.swapaxes(ry[side, x] + ryin[n] + ryin[m], 0, 1)
    for i in (2, 3, 1, 0):
        dy, dc = STEPS_Y[i]
        source = fin_y.at[(yl + dy) % 2, pl.ds(((c + dc) % 2) * COLS, COLS)]
        target = rem.at[:, rows_y(0, 0), :]
        if i == 0:
            fins[8] = pltpu.make_async_copy(source, target, loc_sem.at[7])
        else:
            fins[8 + i] = pltpu.make_async_remote_copy(
                source, target, finy_s.at[i], finy_r.at[i], device_id=dev(dy=dy, dc=dc), device_id_type=MESH
            )
        fins[8 + i].start()
    finish(0)
    fins.pop(0).wait()
    fins.pop(8).wait()
    for copy in fins.values():
        copy.wait_recv()
    proj_ref[...] = app[...] - rem[...]

    groups = [to_same, onward, zs, backs]
    groups += [g.values() for g in (orbs, orbs_y, cols, fwds, cols_y, gathers, sums, ys, xs, fins)]
    for group in groups:
        for copy in group:
            copy.wait_send()


def shards(columns, potential, orbitals):
    f32, bf16 = jnp.float32, jnp.bfloat16
    dma = pltpu.SemaphoreType.DMA
    scratch = [
        pltpu.VMEM((COLS, ROWS, NX), f32),
        pltpu.VMEM((ROWS, NX), f32),
        pltpu.VMEM((2, COLS, ROWS, NX), f32),
        pltpu.VMEM((COLS, ROWS, NX), f32),
        pltpu.VMEM((12 * ORBS, PART, NX), f32),
        pltpu.VMEM((2, 12 * ORBS, PART * NX), bf16),
        pltpu.VMEM((2, 64, PART, NX), f32),
        pltpu.VMEM((2, 128, PART * NX), bf16),
        pltpu.VMEM((12, 2, 8, 128), f32),
        pltpu.VMEM((20, 8, 128), f32),
        pltpu.VMEM((NZ_RING, 8, 128), f32),
        pltpu.VMEM((10, 2, 8, 128), f32),
        pltpu.VMEM((128, 256), bf16),
        pltpu.VMEM((128, 128), bf16),
        pltpu.VMEM((2, NX_RING, PART, 8, NX), f32),
        pltpu.VMEM((NX_RING, PART, 8, NX), f32),
        pltpu.VMEM((NX_RING, 8, PART, NX), f32),
        pltpu.VMEM((2, NX_RING, PART, 8, NX), f32),
        pltpu.VMEM((6, PART, 8, NX), f32),
        pltpu.VMEM((2, PART, 8, NX), f32),
        pltpu.VMEM((2, 8, PART, NX), f32),
        pltpu.VMEM((COLS, ROWS, NX), f32),
        dma((8,)),
        pltpu.SemaphoreType.REGULAR((4,)),
        dma((8,)), dma((8,)),
        dma((16,)), dma((16,)),
        dma((8,)), dma((8,)),
        dma((8,)), dma((8,)),
        dma((4,)), dma((4,)),
        dma((4,)), dma((4,)),
        dma((8,)), dma((8,)),
        dma((20,)), dma((20,)),
        dma((8,)), dma((8,)),
        dma((20,)), dma((20,)),
        dma((4,)), dma((4,)),
        dma((8,)), dma((8,)),
        dma((6,)), dma((6,)),
        dma((4,)), dma((4,)),
    ]
    vmem, anywhere = pl.BlockSpec(memory_space=pltpu.VMEM), pl.BlockSpec(memory_space=pl.ANY)
    projected, correlation = pl.pallas_call(
        kernel,
        out_shape=(
            jax.ShapeDtypeStruct((COLS, ROWS, NX), f32),
            jax.ShapeDtypeStruct((ORBS, 64), f32),
        ),
        in_specs=[anywhere, anywhere, anywhere],
        out_specs=(vmem, vmem),
        scratch_shapes=scratch,
        compiler_params=pltpu.CompilerParams(
            collective_id=0, has_side_effects=True, vmem_limit_bytes=40 * 2**20
        ),
        name="sternheimer",
    )(
        pltpu.with_memory_space_constraint(columns.reshape(COLS, ROWS, NX), pltpu.HBM),
        pltpu.with_memory_space_constraint(potential.reshape(ROWS, NX), pltpu.HBM),
        pltpu.with_memory_space_constraint(orbitals.reshape(ORBS, ROWS, NX), pltpu.HBM),
    )
    return projected.reshape(columns.shape), correlation


def solution(mesh):
    placed = (
        P("band", "space", None, None),
        P("space", None, None),
        P("band", "space", None, None),
    )
    return jax.shard_map(
        shards,
        mesh=mesh,
        in_specs=placed,
        out_specs=(P("band", "space", None, None), P("band", None)),
        check_vma=False,
    )
```

```python
import jax
import jax.numpy as jnp
from jax import lax
from jax.experimental import pallas as pl
from jax.experimental.pallas import tpu as pltpu
from jax.sharding import PartitionSpec as P

COEFFS = (
    -5369.0 / 1800.0,
    12.0 / 7.0,
    -15.0 / 56.0,
    10.0 / 189.0,
    -1.0 / 112.0,
    2.0 / 1925.0,
    -1.0 / 16632.0,
)

MESH = pl.DeviceIdType.MESH
NZ_RING, NX_RING = 8, 4
COLS, ORBS = 4, 32
PLANES, NY, NX = 6, 32, 128
ROWS = PLANES * NY
PART = 16
SPLIT = 8 * PART

STEPS = ((0, 0), (0, 1), (1, 0), (1, 1), (3, 0), (3, 1), (2, 0), (2, 1))
STEPS_Y = ((0, 0), (0, 1), (1, 0), (1, 1))


def kernel(
    col_hbm, pot_hbm, orb_hbm, proj_ref, corr_ref,
    colv, potv, halo, app, phibuf, phi, acol, ahl, cpart, cin, zin, ctot, cts, cts_y,
    rx, rrecv, fin, ry, ryin, rysum, fin_y, rem,
    loc_sem, near_sem, orb_s, orb_r, h_s, h_r, col_s, col_r, fwd_s, fwd_r,
    orby_s, orby_r, coly_s, coly_r, gat_s, gat_r,
    s1_s, s1_r, s2_s, s2_r, s3_s, s3_r, ry_s, ry_r, fin_s, fin_r, rx_s, rx_r, finy_s, finy_r,
):
    s, b = lax.axis_index("space"), lax.axis_index("band")
    z, h = s // 2, s % 2
    x, yl, c = b // 4, (b // 2) % 2, b % 2
    me = x * 2 + c

    def dev(dz=0, dh=0, dx=0, dy=0, dc=0):
        return (
            ((z + dz) % NZ_RING) * 2 + (h + dh) % 2,
            ((x + dx) % NX_RING) * 4 + ((yl + dy) % 2) * 2 + (c + dc) % 2,
        )

    def part_of(dx, dc):
        return ((x + dx) % NX_RING) * 2 + (c + dc) % 2

    def rows_of(g):
        return pl.ds(pl.multiple_of(g * PART, PART), PART)

    def rows_y(dy, dc):
        g = ((yl + dy) % 2) * 2 + (c + dc) % 2
        return pl.ds(pl.multiple_of(SPLIT + g * PART, PART), PART)

    def slot_of(side, g):
        return pl.ds((side * 8 + g) * COLS, COLS)

    def signal(sem, to):
        pl.semaphore_signal(sem, inc=1, device_id=to, device_id_type=MESH)

    partner = dev(dy=1)
    same_z = dev(dh=1)

    barrier = pltpu.get_barrier_semaphore()
    peers = [dev(dx=dx, dc=dc) for dx, dc in STEPS[1:]]
    peers += [partner, dev(dy=1, dc=1), same_z, dev(dz=1), dev(dz=NZ_RING - 1)]
    for peer in peers:
        signal(barrier, peer)

    load_col = pltpu.make_async_copy(col_hbm, colv, loc_sem.at[0])
    load_col.start()
    load_pot = pltpu.make_async_copy(pot_hbm, potv, loc_sem.at[4])
    load_pot.start()
    load_orb = pltpu.make_async_copy(orb_hbm.at[:, rows_of(me), :], phibuf.at[pl.ds(0, ORBS)], loc_sem.at[1])
    load_orb.start()
    load_orb_y = pltpu.make_async_copy(orb_hbm.at[:, rows_y(0, 0), :], phibuf.at[pl.ds(8 * ORBS, ORBS)], loc_sem.at[5])
    load_orb_y.start()

    pl.semaphore_wait(barrier, len(peers))

    signal(near_sem.at[0], dev(dz=1))
    signal(near_sem.at[1], dev(dz=NZ_RING - 1))

    def halo_copy(n, from_here, to, sem):
        j, rows = n // 2, pl.ds(n % 2 * (ROWS // 2), ROWS // 2)
        source = col_hbm.at[j, rows] if from_here else halo.at[1 - h, j, rows]
        return pltpu.make_async_remote_copy(
            source, halo.at[h, j, rows], h_s.at[sem], h_r.at[sem], device_id=to, device_id_type=MESH
        )

    beside = ((z + 1 - 2 * h + NZ_RING) % NZ_RING) * 2 + h, b
    to_same = [halo_copy(n, True, same_z, n) for n in range(2 * COLS)]
    onward = [halo_copy(n, False, beside, 2 * COLS + n) for n in range(2 * COLS)]

    def pass_on(first, last):
        for n in range(first, last):
            to_same[n].wait_recv()
            onward[n].start()
            if n + 4 < 2 * COLS:
                to_same[n + 4].start()

    for copy in to_same[:4]:
        copy.start()

    orbs = {}
    for i, (dx, dc) in enumerate(STEPS):
        if i > 0:
            orbs[i] = pltpu.make_async_remote_copy(
                orb_hbm.at[:, rows_of(part_of(dx, dc)), :],
                phibuf.at[pl.ds(i * ORBS, ORBS)],
                orb_s.at[i],
                orb_r.at[i],
                device_id=dev(dx=dx, dc=dc),
                device_id_type=MESH,
            )
    orbs_y = {}
    for i, (dy, dc) in enumerate(STEPS_Y):
        if i > 0:
            orbs_y[i] = pltpu.make_async_remote_copy(
                orb_hbm.at[:, rows_y(dy, dc), :],
                phibuf.at[pl.ds((8 + i) * ORBS, ORBS)],
                orby_s.at[i],
                orby_r.at[i],
                device_id=dev(dy=dy, dc=dc),
                device_id_type=MESH,
            )
    for i in (2, 4, 3, 5, 1):
        orbs[i].start()
    orbs_y[1].start()
    orbs[6].start()

    load_col.wait()
    load_pot.wait()

    def local_terms(j, carry):
        planes = [colv[j, pl.ds(p * NY, NY), :] for p in range(PLANES)]
        for p in range(PLANES):
            v = planes[p]
            total = (potv[pl.ds(p * NY, NY), :] - 1.5 * COEFFS[0]) * v
            for k in range(1, 7):
                along = pltpu.roll(v, k, 0) + pltpu.roll(v, NY - k, 0)
                along = along + (pltpu.roll(v, k, 1) + pltpu.roll(v, NX - k, 1))
                if p - k >= 0:
                    along = along + planes[p - k]
                if p + k < PLANES:
                    along = along + planes[p + k]
                total = total + (-0.5 * COEFFS[k]) * along
            app[j, pl.ds(p * NY, NY), :] = total
        return carry

    lax.fori_loop(0, 2, local_terms, 0)
    pass_on(0, 2)
    lax.fori_loop(2, COLS, local_terms, 0)
    pass_on(2, 8)

    def split(value):
        high = value.astype(jnp.bfloat16)
        return high, (value - high.astype(jnp.float32)).astype(jnp.bfloat16)

    def lay_out(ref, store, r0, blocks):
        def one(r, carry):
            rows = pl.ds(pl.multiple_of(r0 + r * 16, 16), 16)
            for q0 in range(0, PART, 8):
                high, low = split(jnp.swapaxes(ref[rows, q0 : q0 + 8, :], 0, 1))
                for q in range(8):
                    store(r0 + r * 16, pl.ds((q0 + q) * NX, NX), high[q], low[q])
            return carry

        lax.fori_loop(0, blocks, one, 0)

    def orbitals_to(base, n):
        def store(row, at, high, low):
            k = (row - base) // 16
            rows = pl.ds(pl.multiple_of(base + k % 2 * (n * 16) + k // 2 * 16, 16), 16)
            phi[0, rows, at] = high
            phi[1, rows, at] = low

        return store

    first_rows, last_rows = orbitals_to(0, 8), orbitals_to(256, 4)

    def columns_to(mode):
        def store(row, at, high, low):
            ahl[mode, pl.ds(pl.multiple_of(row, 16), 16), at] = high
            ahl[mode, pl.ds(pl.multiple_of(64 + row, 16), 16), at] = low

        return store

    orbs_y[2].start()
    load_orb.wait()
    orbs[1].wait_recv()
    lay_out(phibuf, first_rows, 0, 4)
    load_orb_y.wait()
    orbs_y[1].wait_recv()
    lay_out(phibuf, last_rows, 256, 4)
    for i in (0, 1):
        pl.semaphore_wait(near_sem.at[i], 1)
    signal(near_sem.at[2], dev(dz=2))
    signal(near_sem.at[3], dev(dz=NZ_RING - 2))

    for copy in onward:
        copy.wait_recv()

    def halo_terms(j, carry):
        for p in range(PLANES):
            total = app[j, pl.ds(p * NY, NY), :]
            for k in range(1, 7):
                if p - k < 0:
                    total = total + (-0.5 * COEFFS[k]) * halo[0, j, pl.ds((p - k + PLANES) * NY, NY), :]
                if p + k >= PLANES:
                    total = total + (-0.5 * COEFFS[k]) * halo[1, j, pl.ds((p + k - PLANES) * NY, NY), :]
            app[j, pl.ds(p * NY, NY), :] = total
        return carry

    lax.fori_loop(0, COLS, halo_terms, 0)

    own_col = pltpu.make_async_copy(app.at[:, rows_of(me), :], acol.at[0, slot_of(yl, me)], loc_sem.at[2])
    own_col.start()
    own_col_y = pltpu.make_async_copy(app.at[:, rows_y(0, 0), :], acol.at[1, slot_of(yl, me)], loc_sem.at[6])
    own_col_y.start()
    cols, fwds, cols_y, gathers = {}, {}, {}, {}
    for i, (dx, dc) in enumerate(STEPS):
        if i > 0:
            cols[i] = pltpu.make_async_remote_copy(
                app.at[:, rows_of(part_of(dx, dc)), :],
                acol.at[0, slot_of(yl, me)],
                col_s.at[i],
                col_r.at[i],
                device_id=dev(dx=dx, dc=dc),
                device_id_type=MESH,
            )
        came = slot_of(yl, part_of(-dx, -dc))
        fwds[i] = pltpu.make_async_remote_copy(
            app.at[:, rows_of(me), :] if i == 0 else acol.at[0, came],
            acol.at[0, came],
            fwd_s.at[i],
            fwd_r.at[i],
            device_id=partner,
            device_id_type=MESH,
        )
    for i, (dy, dc) in enumerate(STEPS_Y):
        if i > 0:
            cols_y[i] = pltpu.make_async_remote_copy(
                app.at[:, rows_y(dy, dc), :],
                acol.at[1, slot_of(yl, me)],
                coly_s.at[i],
                coly_r.at[i],
                device_id=dev(dy=dy, dc=dc),
                device_id_type=MESH,
            )
    def block(dx, dy):
        return acol.at[1, pl.ds(((yl + dy) % 2) * 32 + ((x + dx) % NX_RING) * 8, 8)]

    def gather(n, at, dy, to):
        return pltpu.make_async_remote_copy(
            block(at, dy), block(at, dy), gat_s.at[n], gat_r.at[n], device_id=dev(dx=to), device_id_type=MESH
        )

    for dy in (0, 1):
        gathers[1, dy] = gather(dy, 0, dy, 1)
        gathers[3, dy] = gather(2 + dy, 0, dy, 3)
    gathers[2, 0] = gather(4, 3, 0, 1)
    gathers[2, 1] = gather(5, 1, 1, 3)
    for i in (1, 2, 4, 3, 5, 6, 7):
        cols[i].start()
    for i in (2, 3, 1):
        cols_y[i].start()
    orbs_y[3].start()
    fwds[0].start()
    for i in (2, 4, 3, 5):
        orbs[i].wait_recv()
    lay_out(phibuf, first_rows, 64, 8)
    own_col_y.wait()
    cols_y[1].wait_recv()
    for dx in (1, 3):
        gathers[dx, 0].start()
    for i in (1, 2, 4, 3, 5):
        cols[i].wait_recv()
        fwds[i].start()
    for i in (2, 3):
        cols_y[i].wait_recv()
    for dx in (1, 3):
        gathers[dx, 1].start()
    orbs[7].start()
    gathers[1, 0].wait_recv()
    gathers[2, 0].start()
    for i in (6, 7):
        cols[i].wait_recv()
        fwds[i].start()
    gathers[3, 1].wait_recv()
    gathers[2, 1].start()

    own_col.wait()
    lay_out(acol.at[0], columns_to(0), yl * 32, 2)
    orbs[6].wait_recv()
    lay_out(phibuf, first_rows, 192, 2)
    orbs_y[2].wait_recv()
    lay_out(phibuf, last_rows, 320, 2)
    orbs[7].wait_recv()
    lay_out(phibuf, first_rows, 224, 2)
    orbs_y[3].wait_recv()
    lay_out(phibuf, last_rows, 352, 2)
    for i in range(8):
        fwds[i].wait_recv()
    lay_out(acol.at[0], columns_to(0), 32 - yl * 32, 2)

    half_lanes = lax.broadcasted_iota(jnp.int32, (16, 128), 1) < 64
    dims = (((1,), (1,)), ((), ()))

    def correlate(mode, i0, n):
        rows = pl.ds(i0 * ORBS, n * ORBS)
        high = lax.dot_general(phi[0, rows, :], ahl[mode], dims, preferred_element_type=jnp.float32)
        low = lax.dot_general(phi[1, rows, :], ahl[mode], dims, preferred_element_type=jnp.float32)
        value = high + pltpu.roll(high, 64, 1) + low
        for i in range(n):
            first = value[i * 16 : i * 16 + 16]
            second = value[(n + i) * 16 : (n + i) * 16 + 16]
            packed = jnp.where(half_lanes, first, pltpu.roll(second, 64, 1))
            if i0 + i in (8, 9):
                cpart[i0 + i - 8, 0] += packed[:8]
                cpart[i0 + i - 8, 1] += packed[8:]
            else:
                cpart[i0 + i, 0] = packed[:8]
                cpart[i0 + i, 1] = packed[8:]

    sums = {}

    def send_parts(i):
        if i < 8:
            dx, dc = STEPS[i]
            dy, n0 = 0, i * 2
        else:
            dx, (dy, dc) = 0, STEPS_Y[i - 8]
            n0 = i * 2 - 4
        for dh in (0, 1):
            if (i, dh) != (0, 0):
                n = n0 + dh
                sums[n] = pltpu.make_async_remote_copy(
                    cpart.at[i, (h + dh) % 2],
                    cin.at[n],
                    s1_s.at[n],
                    s1_r.at[n],
                    device_id=dev(dx=-dx, dy=dy, dc=-dc, dh=dh),
                    device_id_type=MESH,
                )
                sums[n].start()

    correlate(0, 0, 8)
    for i in (6, 7, 2, 4, 3, 5):
        send_parts(i)
    for n in ((3, 0), (2, 0)):
        gathers[n].wait_recv()
    lay_out(acol.at[1], columns_to(1), yl * 32, 2)
    for n in ((1, 1), (2, 1)):
        gathers[n].wait_recv()
    lay_out(acol.at[1], columns_to(1), 32 - yl * 32, 2)
    correlate(1, 8, 4)
    for i in (10, 11, 1, 0):
        send_parts(i)

    total = cpart[0, h]
    for n in range(1, 20):
        sums[n].wait_recv()
        total = total + cin[n]

    zin[z] = total
    for i in (2, 3):
        pl.semaphore_wait(near_sem.at[i], 1)
    zs = []
    for dz in (4, 3, 5, 2, 6, 1, 7):
        copy = pltpu.make_async_remote_copy(
            zin.at[z], zin.at[z], s2_s.at[dz], s2_r.at[dz], device_id=dev(dz=dz), device_id_type=MESH
        )
        copy.start()
        zs.append(copy)
    for copy in zs:
        copy.wait_recv()
    total = zin[0]
    for n in range(1, NZ_RING):
        total = total + zin[n]

    ctot[0, h] = total
    backs = []
    users = [(i, dx, 0, dc) for i, (dx, dc) in enumerate(STEPS)]
    users += [(8, 0, 1, 0), (9, 0, 1, 1)]
    for i in (6, 7, 8, 9, 2, 4, 3, 5, 1, 0):
        _, dx, dy, dc = users[i]
        for dh in (1, 0):
            if (i, dh) != (0, 0):
                n = i * 2 + dh
                copy = pltpu.make_async_remote_copy(
                    ctot.at[0, h],
                    ctot.at[i, h],
                    s3_s.at[n],
                    s3_r.at[n],
                    device_id=dev(dx=dx, dy=dy, dc=dc, dh=dh),
                    device_id_type=MESH,
                )
                copy.start()
                backs.append(copy)
    for copy in backs:
        copy.wait_recv()

    def operand(packed, out):
        high, low = split(packed)
        out[pl.ds(0, 64), :] = high
        out[pl.ds(64, 64), :] = low

    def removed(left, rows, out):
        for q0 in range(0, PART, 4):
            at = pl.ds(q0 * NX, 4 * NX)
            both = jnp.dot(left[...], phi[0, rows, at], preferred_element_type=jnp.float32)
            rest = jnp.dot(left[pl.ds(0, 64), :], phi[1, rows, at], preferred_element_type=jnp.float32)
            value = both[:64] + both[64:] + rest
            for q in range(4):
                for side in (0, 1):
                    for k in range(NX_RING):
                        n = side * 32 + k * 8
                        out[side, k, q0 + q] = value[n : n + 8, q * NX : (q + 1) * NX]

    packed = jnp.concatenate([ctot[0:2].reshape(32, 128), ctot[8:10].reshape(32, 128)], axis=0)
    turned = jnp.transpose(jnp.concatenate([packed, packed], axis=0))
    low_lanes = lax.broadcasted_iota(jnp.int32, (64, 128), 1) < 64
    operand(jnp.where(low_lanes, turned[:64], turned[64:]), cts_y)
    removed(cts_y, pl.ds(256, 128), ry)

    def along_x(n, source, dx):
        return pltpu.make_async_remote_copy(
            source, ryin.at[n], rx_s.at[n], rx_r.at[n], device_id=dev(dx=dx), device_id_type=MESH
        )

    up, down = (x + 1) % NX_RING, (x + 3) % NX_RING
    xs = {
        0: along_x(0, ry.at[0, (x + 2) % NX_RING], 1),
        1: along_x(1, ry.at[1, (x + 2) % NX_RING], 3),
        2: along_x(2, ry.at[1, up], 1),
        3: along_x(3, ry.at[0, down], 3),
        4: along_x(4, rysum.at[0], 1),
        5: along_x(5, rysum.at[1], 3),
    }
    for n in range(4):
        xs[n].start()

    turned = jnp.transpose(ctot[0:8].reshape(128, 128))
    operand(jnp.concatenate([turned[:64], turned[64:]], axis=1), cts)
    removed(cts, pl.ds(0, 256), rx)
    order = (2, 1, 3, 0)
    ys = {}
    for dx in order:
        k = (x + dx) % NX_RING
        ys[dx] = pltpu.make_async_remote_copy(
            rx.at[1 - yl, k], rrecv.at[k], ry_s.at[dx], ry_r.at[dx], device_id=partner, device_id_type=MESH
        )
        ys[dx].start()
    for n, to in ((0, up), (1, down)):
        xs[n].wait_recv()
        rysum[n] = ry[n, to] + ryin[n]
        xs[4 + n].start()

    packed = ctot[0].reshape(16, 128)
    own = jnp.concatenate([packed, pltpu.roll(packed, 64, 1)], axis=0)
    lane = lax.broadcasted_iota(jnp.int32, (ORBS, 128), 1)
    value = own
    for side in (0, 1):
        for k in range(NX_RING):
            source, target = side * 32 + k * 8, k * 16 + side * 8
            if source != target:
                moved = pltpu.roll(own, (target - source) % 128, 1)
                value = jnp.where((lane >= target) & (lane < target + 8), moved, value)
    corr_ref[...] = value[:, :64]

    fins = {}

    def finish(dx):
        k = (x + dx) % NX_RING
        ys[dx].wait_recv()
        fin[k] = jnp.swapaxes(rx[yl, k] + rrecv[k], 0, 1)
        for dc in (1, 0):
            source = fin.at[k, pl.ds(((c + dc) % 2) * COLS, COLS)]
            target = rem.at[:, rows_of(me), :]
            n = STEPS.index((dx, dc))
            if n == 0:
                fins[n] = pltpu.make_async_copy(source, target, loc_sem.at[3])
            else:
                fins[n] = pltpu.make_async_remote_copy(
                    source, target, fin_s.at[n], fin_r.at[n], device_id=dev(dx=dx, dc=dc), device_id_type=MESH
                )
            fins[n].start()

    for dx in order[:3]:
        finish(dx)
    for side, n, m in ((0, 3, 4), (1, 2, 5)):
        xs[n].wait_recv()
        xs[m].wait_recv()
        fin_y[side] = jnp.swapaxes(ry[side, x] + ryin[n] + ryin[m], 0, 1)
    for i in (2, 3, 1, 0):
        dy, dc = STEPS_Y[i]
        source = fin_y.at[(yl + dy) % 2, pl.ds(((c + dc) % 2) * COLS, COLS)]
        target = rem.at[:, rows_y(0, 0), :]
        if i == 0:
            fins[8] = pltpu.make_async_copy(source, target, loc_sem.at[7])
        else:
            fins[8 + i] = pltpu.make_async_remote_copy(
                source, target, finy_s.at[i], finy_r.at[i], device_id=dev(dy=dy, dc=dc), device_id_type=MESH
            )
        fins[8 + i].start()
    finish(0)
    fins.pop(0).wait()
    fins.pop(8).wait()
    for copy in fins.values():
        copy.wait_recv()
    proj_ref[...] = app[...] - rem[...]

    groups = [to_same, onward, zs, backs]
    groups += [g.values() for g in (orbs, orbs_y, cols, fwds, cols_y, gathers, sums, ys, xs, fins)]
    for group in groups:
        for copy in group:
            copy.wait_send()


def shards(columns, potential, orbitals):
    f32, bf16 = jnp.float32, jnp.bfloat16
    dma = pltpu.SemaphoreType.DMA
    scratch = [
        pltpu.VMEM((COLS, ROWS, NX), f32),
        pltpu.VMEM((ROWS, NX), f32),
        pltpu.VMEM((2, COLS, ROWS, NX), f32),
        pltpu.VMEM((COLS, ROWS, NX), f32),
        pltpu.VMEM((12 * ORBS, PART, NX), f32),
        pltpu.VMEM((2, 12 * ORBS, PART * NX), bf16),
        pltpu.VMEM((2, 64, PART, NX), f32),
        pltpu.VMEM((2, 128, PART * NX), bf16),
        pltpu.VMEM((12, 2, 8, 128), f32),
        pltpu.VMEM((20, 8, 128), f32),
        pltpu.VMEM((NZ_RING, 8, 128), f32),
        pltpu.VMEM((10, 2, 8, 128), f32),
        pltpu.VMEM((128, 256), bf16),
        pltpu.VMEM((128, 128), bf16),
        pltpu.VMEM((2, NX_RING, PART, 8, NX), f32),
        pltpu.VMEM((NX_RING, PART, 8, NX), f32),
        pltpu.VMEM((NX_RING, 8, PART, NX), f32),
        pltpu.VMEM((2, NX_RING, PART, 8, NX), f32),
        pltpu.VMEM((6, PART, 8, NX), f32),
        pltpu.VMEM((2, PART, 8, NX), f32),
        pltpu.VMEM((2, 8, PART, NX), f32),
        pltpu.VMEM((COLS, ROWS, NX), f32),
        dma((8,)),
        pltpu.SemaphoreType.REGULAR((4,)),
        dma((8,)), dma((8,)),
        dma((16,)), dma((16,)),
        dma((8,)), dma((8,)),
        dma((8,)), dma((8,)),
        dma((4,)), dma((4,)),
        dma((4,)), dma((4,)),
        dma((8,)), dma((8,)),
        dma((20,)), dma((20,)),
        dma((8,)), dma((8,)),
        dma((20,)), dma((20,)),
        dma((4,)), dma((4,)),
        dma((8,)), dma((8,)),
        dma((6,)), dma((6,)),
        dma((4,)), dma((4,)),
    ]
    vmem, anywhere = pl.BlockSpec(memory_space=pltpu.VMEM), pl.BlockSpec(memory_space=pl.ANY)
    projected, correlation = pl.pallas_call(
        kernel,
        out_shape=(
            jax.ShapeDtypeStruct((COLS, ROWS, NX), f32),
            jax.ShapeDtypeStruct((ORBS, 64), f32),
        ),
        in_specs=[anywhere, anywhere, anywhere],
        out_specs=(vmem, vmem),
        scratch_shapes=scratch,
        compiler_params=pltpu.CompilerParams(
            collective_id=0, has_side_effects=True, vmem_limit_bytes=40 * 2**20
        ),
        name="sternheimer",
    )(
        pltpu.with_memory_space_constraint(columns.reshape(COLS, ROWS, NX), pltpu.HBM),
        pltpu.with_memory_space_constraint(potential.reshape(ROWS, NX), pltpu.HBM),
        pltpu.with_memory_space_constraint(orbitals.reshape(ORBS, ROWS, NX), pltpu.HBM),
    )
    return projected.reshape(columns.shape), correlation


def solution(mesh):
    placed = (
        P("band", "space", None, None),
        P("space", None, None),
        P("band", "space", None, None),
    )
    return jax.shard_map(
        shards,
        mesh=mesh,
        in_specs=placed,
        out_specs=(P("band", "space", None, None), P("band", None)),
        check_vma=False,
    )
```
